32 devices in a mesh: group: 2 (over y), tensor: 4 (over z), seq: 4 (over x, core).
Axes of the slice: x: 2, y: 2, z: 4, core: 2. Of those that a mesh axis runs over, the one named last changes fastest.
Arguments:
- tokens: bfloat16 [5120, 3584], P(('group', 'seq', 'tensor')), parts along dimension 0, may hold values from -24 to 24
- cotangent: bfloat16 [5120, 3584], P(('group', 'seq', 'tensor')), parts along dimension 0, may hold values from -6 to 6
- modulation: float32 [6, 3584], P('group'), parts along dimension 0, may hold values from -1 to 1
- w_qkv: bfloat16 [3584, 3, 512], P(None, None, 'tensor'), may hold values from -0.09375 to 0.09375
- w_out: bfloat16 [512, 3584], P('tensor'), may hold values from -0.25 to 0.25
- qk_gain: float32 [2, 128], replicated, may hold values from 0.5 to 3
Outputs:
- input_grad: float32 [5120, 3584], P(('group', 'seq', 'tensor')), parts along dimension 0
The draws below stay inside these ranges and needn't reach their ends.
There are 2 independent parts, one for each index of `group`. The reference program is written for one: setup_inputs(seed, part) draws one part's arguments, and reference() takes and returns one part's arrays. A program takes and returns all parts, laid end to end along the dimension named above; an argument that names none is the same for every part. Nothing has to cross between parts.
All inputs are finite; a program needn't handle non-finite values.
Results may differ from the reference program's by a relative error of at most 0.019.
Values may be sent and summed in bfloat16 or wider, within the bound.
No kernel may reach another device: no remote copies, remote signals or barrier semaphores. Data moves between devices by JAX's collectives and lax.ppermute only.
A program may use at most 64 MiB of HBM per device.

```python
import math
import jax
import jax.numpy as jnp
from jax import lax

D = 3584
HEAD_DIM = 128
HEAD_DEV = 1
HEADS = 4
SEQLEN = 2560
N_TENSOR = 4


def draw_tokens(key, part):
    key = jax.random.fold_in(key, 5)
    first, second, third = jax.random.split(key, 3)
    base = jnp.clip(jax.random.normal(first, (SEQLEN, D), jnp.float32), -4.0, 4.0)
    columns = jnp.exp(jax.random.uniform(second, (D,), jnp.float32, math.log(0.3), math.log(3.0)))
    rows = jnp.exp(jax.random.uniform(third, (SEQLEN, 1), jnp.float32, math.log(0.4), math.log(2.0)))
    return (base * columns * rows).astype(jnp.bfloat16)


def draw_qk_gain(key, part):
    key = jax.random.fold_in(key, 11)
    first = jax.random.fold_in(key, 0)
    gains = jax.random.uniform(first, (2, HEAD_DIM), jnp.float32, 0.5, 2.2)
    return gains


def level_of(key, shape, pieces, smallest, high):
    loudness, own = 1.0, jax.random.fold_in(key, 6)
    for axis_at, parts in pieces:
        steps = jnp.exp(jax.random.uniform(jax.random.fold_in(own, axis_at), (parts,), jnp.float32, smallest / len(pieces), high / len(pieces)))
        loudness = loudness * jnp.repeat(steps, shape[axis_at] // parts).reshape([-1 if axis == axis_at else 1 for axis in range(len(shape))])
    return loudness


def bell_draw(rng, extent, spread, reach, pieces=(), kind=jnp.bfloat16):
    loudness = level_of(rng, extent, pieces, -0.22, 0.18) if pieces else 1.0
    drawn = jax.random.normal(rng, extent, jnp.float32) * spread * loudness
    return jnp.minimum(jnp.maximum(drawn, -reach), reach).astype(kind)


def setup_inputs(seed: int = 0, part: int = 0) -> dict:
    splits = jax.random.split(jax.random.key(seed), 7)
    part_splits = jax.random.split(jax.random.fold_in(splits[6], part), 7)
    tokens = draw_tokens(jax.random.fold_in(jax.random.fold_in(splits[6], part), 71), part)
    cotangent = bell_draw(part_splits[1], (SEQLEN, D), 1.0, 6.0, ((0, 16),))
    modulation = jnp.clip(jax.random.uniform(part_splits[2], (3, D), jnp.float32, -1.0, 1.0), -1.0, 1.0)
    w_qkv = bell_draw(splits[3], (D, 3, HEADS * HEAD_DIM), D ** -0.5, 0.09375, ((2, 4),))
    w_out = bell_draw(splits[4], (HEADS * HEAD_DIM, D), (HEADS * HEAD_DIM) ** -0.5, 0.25, ((0, 4),))
    qk_gain = draw_qk_gain(jax.random.fold_in(splits[6], 71), part)
    return {"tokens": tokens, "cotangent": cotangent, "modulation": modulation, "w_qkv": w_qkv, "w_out": w_out, "qk_gain": qk_gain}


def head_norm(raw, gain):
    scale_back = lax.rsqrt(lax.optimization_barrier(jnp.mean(raw * raw, axis=-1, keepdims=True)) + 1e-06)
    return (raw * scale_back * gain, scale_back)

def head_norm_back(raw, scale_back, gain, upstream):
    scaled_up = upstream * gain
    return scale_back * scaled_up - raw * scale_back ** 3 * lax.optimization_barrier(jnp.mean(raw * scaled_up, axis=-1, keepdims=True))

def reference(tokens, cotangent, modulation, w_qkv, w_out, qk_gain):
    width = HEAD_DEV * HEAD_DIM
    all_width = HEADS * HEAD_DIM
    inv_sqrt = 1.0 / math.sqrt(HEAD_DIM)
    modulation_shift = modulation[0]
    modulation_scale = modulation[1]
    gate = modulation[2]
    input_rows_all = tokens.astype(jnp.float32)
    inverse_stddev = lax.rsqrt(lax.optimization_barrier(jnp.mean(input_rows_all * input_rows_all, axis=-1, keepdims=True)) + 1e-06)
    centered_normalized = input_rows_all * inverse_stddev
    layer_normed = (centered_normalized * (1.0 + modulation_scale) + modulation_shift).astype(jnp.bfloat16)
    qkv = jnp.dot(layer_normed, w_qkv.reshape(D, 3 * all_width), preferred_element_type=jnp.float32)
    query = qkv[:, :all_width].reshape(SEQLEN, HEADS, HEAD_DIM)
    keys = qkv[:, all_width:2 * all_width].reshape(SEQLEN, HEADS, HEAD_DIM)
    values = qkv[:, 2 * all_width:].reshape(SEQLEN, HEADS, HEAD_DIM)
    query_n, query_rs = head_norm(query, qk_gain[0])
    keys_n, keys_rs = head_norm(keys, qk_gain[1])
    query_b = query_n.astype(jnp.bfloat16)
    keys_b = keys_n.astype(jnp.bfloat16)
    values_b = values.astype(jnp.bfloat16)
    scaled = (cotangent.astype(jnp.float32) * gate).astype(jnp.bfloat16)
    dattn = lax.dot_general(scaled, w_out, (((1,), (1,)), ((), ())), preferred_element_type=jnp.float32)
    dattn_b = dattn.astype(jnp.bfloat16).reshape(SEQLEN, HEADS, HEAD_DIM)

    def one_head(items):
        qh, kh, vh, gh = items
        scores = jnp.dot(qh, kh.T, preferred_element_type=jnp.float32) * inv_sqrt
        row_max = lax.optimization_barrier(jnp.max(scores, axis=-1, keepdims=True))
        expo = jnp.exp(scores - row_max)
        row_sum = lax.optimization_barrier(jnp.sum(expo, axis=-1, keepdims=True))
        probs = expo / row_sum
        probs_b = probs.astype(jnp.bfloat16)
        attn_b = jnp.dot(probs_b, vh, preferred_element_type=jnp.float32).astype(jnp.bfloat16)
        delta = lax.optimization_barrier(jnp.sum(gh.astype(jnp.float32) * attn_b.astype(jnp.float32), axis=-1, keepdims=True))
        dprob = jnp.dot(gh, vh.T, preferred_element_type=jnp.float32)
        dscore = (probs * (dprob - delta)).astype(jnp.bfloat16)
        dquery = jnp.dot(dscore, kh, preferred_element_type=jnp.float32) * inv_sqrt
        dkey = jnp.dot(dscore.T, qh, preferred_element_type=jnp.float32) * inv_sqrt
        dvalue = jnp.dot(probs_b.T, gh, preferred_element_type=jnp.float32)
        return (dquery, dkey, dvalue)
    heads_first = (jnp.transpose(query_b, (1, 0, 2)), jnp.transpose(keys_b, (1, 0, 2)), jnp.transpose(values_b, (1, 0, 2)), jnp.transpose(dattn_b, (1, 0, 2)))
    dquery, dkey, dvalue = lax.map(one_head, heads_first)
    dquery = jnp.transpose(dquery, (1, 0, 2))
    dkey = jnp.transpose(dkey, (1, 0, 2))
    dvalue = jnp.transpose(dvalue, (1, 0, 2))
    dq_raw = head_norm_back(query, query_rs, qk_gain[0], dquery)
    dk_raw = head_norm_back(keys, keys_rs, qk_gain[1], dkey)
    dqkv = jnp.stack([dq_raw.reshape(SEQLEN, all_width), dk_raw.reshape(SEQLEN, all_width), dvalue.reshape(SEQLEN, all_width)], axis=1).astype(jnp.bfloat16)
    grouped = jnp.moveaxis(dqkv.reshape(SEQLEN, 3, N_TENSOR, width), 2, 0)
    weights_grouped = jnp.moveaxis(w_qkv.reshape(D, 3, N_TENSOR, width), 2, 0)

    def add_group(total, items):
        part, wpart = items
        term = lax.dot_general(part.reshape(SEQLEN, 3 * width), wpart.reshape(D, 3 * width), (((1,), (1,)), ((), ())), preferred_element_type=jnp.float32)
        term_b = lax.optimization_barrier(term.astype(jnp.bfloat16))
        return (total + term_b.astype(jnp.float32), None)
    dnormed, _ = lax.scan(add_group, jnp.zeros((SEQLEN, D), jnp.float32), (grouped, weights_grouped))
    normalized_grad = dnormed * (1.0 + modulation_scale)
    final_output = cotangent.astype(jnp.float32) + inverse_stddev * (normalized_grad - centered_normalized * lax.optimization_barrier(jnp.mean(normalized_grad * centered_normalized, axis=-1, keepdims=True)))
    return final_output
```

```python
import math
from functools import partial

import jax
import jax.numpy as jnp
from jax import lax
from jax.experimental import pallas as pl
from jax.experimental.pallas import tpu as pltpu
from jax.sharding import PartitionSpec as P


def head_norm(raw, gain):
    scale_back = lax.rsqrt(jnp.mean(raw * raw, axis=-1, keepdims=True) + 1e-06)
    return (raw * scale_back * gain, scale_back)


def head_norm_back(raw, scale_back, gain, upstream):
    scaled_up = upstream * gain
    return scale_back * scaled_up - raw * scale_back**3 * jnp.mean(
        raw * scaled_up, axis=-1, keepdims=True
    )


def token_gather_body(tokens, cotangent, modulation, w_qkv, w_out, qk_gain):
    head_dim = qk_gain.shape[1]
    width = w_out.shape[0]
    nheads = width // head_dim
    model_width = tokens.shape[1]
    inv_sqrt = 1.0 / math.sqrt(head_dim)
    modulation_shift = modulation[0]
    modulation_scale = modulation[1]
    gate = modulation[2]
    input_rows_all = tokens.astype(jnp.float32)
    inverse_stddev = lax.rsqrt(
        jnp.mean(input_rows_all * input_rows_all, axis=-1, keepdims=True) + 1e-06
    )
    centered_normalized = input_rows_all * inverse_stddev
    layer_normed = (centered_normalized * (1.0 + modulation_scale) + modulation_shift).astype(
        jnp.bfloat16
    )
    cotangent_rows_all = cotangent.astype(jnp.float32)
    scaled_grad = (cotangent_rows_all * gate).astype(jnp.bfloat16)
    flat_in = w_qkv.reshape(model_width, 3 * width)
    qkv = jnp.dot(
        lax.all_gather(layer_normed, "tensor", axis=0, tiled=True),
        flat_in,
        preferred_element_type=jnp.float32,
    )
    rows = qkv.shape[0]
    query = qkv[:, :width].reshape(rows, nheads, head_dim)
    keys = qkv[:, width : 2 * width].reshape(rows, nheads, head_dim)
    values = qkv[:, 2 * width :].reshape(rows, nheads, head_dim)
    query_n, query_rs = head_norm(query, qk_gain[0])
    keys_n, keys_rs = head_norm(keys, qk_gain[1])
    query_b = query_n.astype(jnp.bfloat16)
    keys_b = keys_n.astype(jnp.bfloat16).reshape(rows, width)
    values_b = values.astype(jnp.bfloat16).reshape(rows, width)
    keys_all, values_all = (
        lax.all_gather(keys_b, "seq", axis=0, tiled=True),
        lax.all_gather(values_b, "seq", axis=0, tiled=True),
    )
    total = keys_all.shape[0]
    block = min(total, 512)
    count_blocks = total // block
    key_stack = keys_all.reshape(count_blocks, block, nheads, head_dim)
    value_stack = values_all.reshape(count_blocks, block, nheads, head_dim)

    def block_scores(queries, block_keys):
        return (
            jnp.einsum("qhd,khd->hqk", queries, block_keys, preferred_element_type=jnp.float32)
            * inv_sqrt
        )

    def stats_step(carry, block_keys):
        row_max, row_sum = carry
        scores = block_scores(query_b, block_keys)
        new_max = jnp.maximum(row_max, jnp.max(scores, axis=-1))
        row_sum = row_sum * jnp.exp(row_max - new_max) + jnp.sum(
            jnp.exp(scores - new_max[..., None]), axis=-1
        )
        return ((new_max, row_sum), None)

    start_max = jnp.full((nheads, rows), -jnp.inf, jnp.float32)
    start_sum = jnp.zeros((nheads, rows), jnp.float32)
    (row_max, row_sum), _ = lax.scan(stats_step, (start_max, start_sum), key_stack)

    def probs_of(scores, bmax, bsum):
        return jnp.exp(scores - bmax[..., None]) / bsum[..., None]

    def output_step(acc, pair):
        weights_b = probs_of(block_scores(query_b, pair[0]), row_max, row_sum).astype(jnp.bfloat16)
        return (
            acc
            + jnp.einsum("hqk,khd->hqd", weights_b, pair[1], preferred_element_type=jnp.float32),
            None,
        )

    attn_acc, _ = lax.scan(
        output_step, jnp.zeros((nheads, rows, head_dim), jnp.float32), (key_stack, value_stack)
    )
    attn_b = attn_acc.astype(jnp.bfloat16)
    dout = lax.dot_general(
        lax.all_gather(scaled_grad, "tensor", axis=0, tiled=True),
        w_out,
        (((1,), (1,)), ((), ())),
        preferred_element_type=jnp.float32,
    )
    grad_b = dout.astype(jnp.bfloat16)
    grad_q = grad_b.reshape(rows, nheads, head_dim)
    delta = jnp.sum(
        jnp.transpose(grad_q, (1, 0, 2)).astype(jnp.float32) * attn_b.astype(jnp.float32), axis=-1
    )

    def grad_terms(queries, grads, block_keys, block_values, bmax, bsum, bdelta):
        weights = probs_of(block_scores(queries, block_keys), bmax, bsum)
        dprob = jnp.einsum("qhd,khd->hqk", grads, block_values, preferred_element_type=jnp.float32)
        dscore = (weights * (dprob - bdelta[..., None])).astype(jnp.bfloat16)
        return (weights.astype(jnp.bfloat16), dscore)

    zeros_heads = jnp.zeros((nheads, rows, head_dim), jnp.float32)

    def both_step(acc, pair):
        weights_b, dscore = grad_terms(query_b, grad_q, pair[0], pair[1], row_max, row_sum, delta)
        acc = (
            acc
            + jnp.einsum("hqk,khd->hqd", dscore, pair[0], preferred_element_type=jnp.float32)
            * inv_sqrt
        )
        dkey_part = (
            jnp.einsum("hqk,qhd->khd", dscore, query_b, preferred_element_type=jnp.float32)
            * inv_sqrt
        )
        dvalue_part = jnp.einsum(
            "hqk,qhd->khd", weights_b, grad_q, preferred_element_type=jnp.float32
        )
        return (
            acc,
            jnp.concatenate(
                [dkey_part.reshape(block, width), dvalue_part.reshape(block, width)], axis=1
            ),
        )

    dquery, key_terms = lax.scan(both_step, zeros_heads, (key_stack, value_stack))
    own_terms = lax.psum_scatter(
        key_terms.reshape(total, 2 * width).astype(jnp.bfloat16),
        "seq",
        scatter_dimension=0,
        tiled=True,
    ).astype(jnp.float32)
    dkey = own_terms[:, :width].reshape(rows, nheads, head_dim)
    dvalue = own_terms[:, width:].reshape(rows, nheads, head_dim)
    dquery = jnp.transpose(dquery, (1, 0, 2))
    dq_raw = head_norm_back(query, query_rs, qk_gain[0], dquery)
    dk_raw = head_norm_back(keys, keys_rs, qk_gain[1], dkey)
    dqkv = jnp.concatenate(
        [dq_raw.reshape(rows, width), dk_raw.reshape(rows, width), dvalue.reshape(rows, width)],
        axis=1,
    ).astype(jnp.bfloat16)
    dnormed = lax.psum_scatter(
        lax.dot_general(
            dqkv, flat_in, (((1,), (1,)), ((), ())), preferred_element_type=jnp.float32
        ).astype(jnp.bfloat16),
        "tensor",
        scatter_dimension=0,
        tiled=True,
    ).astype(jnp.float32)
    normalized_grad = dnormed * (1.0 + modulation_scale)
    final_output = cotangent_rows_all + inverse_stddev * (
        normalized_grad
        - centered_normalized
        * jnp.mean(normalized_grad * centered_normalized, axis=-1, keepdims=True)
    )
    return final_output


CORE_SWAP = [(0, 1), (1, 0), (2, 3), (3, 2)]
CHIP_SWAP = [(0, 2), (2, 0), (1, 3), (3, 1)]
PLANE = ("group", "seq")


def plane_swap(first):
    pairs = []
    for group in range(2):
        for seq in range(4):
            along_chip = (seq % 2 == 0) == first
            to = group * 4 + (seq ^ 2) if along_chip else (1 - group) * 4 + seq
            pairs.append((group * 4 + seq, to))
    return pairs


def around(value, step, count):
    return lax.ppermute(value, "tensor", [(i, (i + step) % count) for i in range(count)])


def attention_kernel(
    scale, block, q_ref, g_ref, k_ref, v_ref, dq_ref, dk_ref, dv_ref, score_ref, prob_ref, dprob_ref
):
    total = k_ref.shape[0]
    rows, dim = q_ref.shape
    steps = total // block
    nt = (((1,), (1,)), ((), ()))
    tn = (((0,), (0,)), ((), ()))

    def scores(i, top):
        here = pl.ds(pl.multiple_of(i * block, block), block)
        s = lax.dot_general(k_ref[here, :], q_ref[...], nt, preferred_element_type=jnp.float32) * scale
        score_ref[here, :] = s
        dprob_ref[here, :] = lax.dot_general(
            v_ref[here, :], g_ref[...], nt, preferred_element_type=jnp.float32
        )
        return jnp.maximum(top, jnp.max(s, axis=0, keepdims=True))

    top = lax.fori_loop(0, steps, scores, jnp.full((1, rows), -jnp.inf, jnp.float32))

    def weigh(i, carry):
        norm, cross = carry
        here = pl.ds(pl.multiple_of(i * block, block), block)
        e = jnp.exp(score_ref[here, :] - top)
        prob_ref[here, :] = e
        return (
            norm + jnp.sum(e, axis=0, keepdims=True),
            cross + jnp.sum(e * dprob_ref[here, :], axis=0, keepdims=True),
        )

    none = jnp.zeros((1, rows), jnp.float32)
    norm, cross = lax.fori_loop(0, steps, weigh, (none, none))
    inverse = 1.0 / norm
    delta = cross * inverse

    def back(i, dq):
        here = pl.ds(pl.multiple_of(i * block, block), block)
        p = prob_ref[here, :] * inverse
        ds = (p * (dprob_ref[here, :] - delta)).astype(jnp.bfloat16)
        dk_ref[here, :] = (
            jnp.dot(ds, q_ref[...], preferred_element_type=jnp.float32) * scale
        )
        dv_ref[here, :] = jnp.dot(
            p.astype(jnp.bfloat16), g_ref[...], preferred_element_type=jnp.float32
        )
        return dq + lax.dot_general(k_ref[here, :], ds, tn, preferred_element_type=jnp.float32)

    dq = lax.fori_loop(0, steps, back, jnp.zeros((dim, rows), jnp.float32))
    dq_ref[...] = dq.T * scale


def attention(q, g, k, v):
    rows, dim = q.shape
    total = k.shape[0]
    f32 = jnp.float32
    vmem = pl.BlockSpec(memory_space=pltpu.VMEM)
    work = rows * total * dim
    return pl.pallas_call(
        partial(attention_kernel, 1.0 / math.sqrt(dim), 256),
        out_shape=(
            jax.ShapeDtypeStruct((rows, dim), f32),
            jax.ShapeDtypeStruct((total, dim), f32),
            jax.ShapeDtypeStruct((total, dim), f32),
        ),
        in_specs=[vmem] * 4,
        out_specs=(vmem,) * 3,
        scratch_shapes=[pltpu.VMEM((total, rows), f32)] * 3,
        compiler_params=pltpu.CompilerParams(vmem_limit_bytes=48 * 1024 * 1024),
        cost_estimate=pl.CostEstimate(
            flops=10 * work, bytes_accessed=16 * total * dim, transcendentals=rows * total
        ),
        name="attention",
    )(q, g, k, v)


def weight_gather_body(count, tokens, cotangent, modulation, w_qkv, w_out, qk_gain):
    bf16, f32 = jnp.bfloat16, jnp.float32
    dim = qk_gain.shape[1]
    rows, width = tokens.shape
    half = width // 2
    part = half // 4
    seq = lax.axis_index("seq")
    core, chip, group = seq % 2, seq // 2, lax.axis_index("group")
    this = core * half
    other = half - this
    mine = 2 * group + chip
    across = 2 * group + (1 - chip)
    over = 2 * (1 - group) + chip
    far = 3 - mine
    first = jnp.where(core == 0, across, over)
    second = jnp.where(core == 0, over, across)

    def assemble(pieces):
        whole = jnp.zeros((half, pieces[0].shape[1]), bf16)
        for place, piece in pieces_at(pieces):
            whole = lax.dynamic_update_slice(whole, piece, (place * part, 0))
        return whole

    def pieces_at(pieces):
        own, one, pair = pieces
        return ((mine, own), (first, one), (second, pair[:part]), (far, pair[part:]))

    def hand_round(own):
        one = lax.ppermute(own, PLANE, plane_swap(True))
        pair = lax.ppermute(jnp.concatenate([own, one], axis=0), PLANE, plane_swap(False))
        return assemble((own, one, pair))

    own_in = lax.dynamic_slice(w_qkv, (this + mine * part, 0, 0), (part, 3, dim)).reshape(part, 3 * dim)
    own_out = lax.dynamic_slice(w_out, (0, this + mine * part), (dim, part)).T
    w_in_half = lax.dynamic_slice(w_qkv, (this, 0, 0), (half, 3, dim)).reshape(half, 3 * dim)
    w_out_half = lax.dynamic_slice(w_out, (0, this), (dim, half)).T
    order = [1, count - 1] + list(range(2, count - 1))
    w_in = {0: w_in_half}
    w_o = {0: w_out_half}
    for step in order:
        w_in[step] = hand_round(around(own_in, step, count))
    for step in order:
        w_o[step] = hand_round(around(own_out, step, count))

    shift, scale, gate = modulation[0], 1.0 + modulation[1], modulation[2]
    x = tokens.astype(f32)
    inv = lax.rsqrt(jnp.mean(x * x, axis=-1, keepdims=True) + 1e-06)
    xhat = x * inv
    normed = (xhat * scale + shift).astype(bf16)
    cot = cotangent.astype(f32)
    scaled = (cot * gate).astype(bf16)

    def both_cores(value):
        keep = lax.dynamic_slice(value, (0, this), (rows, half))
        send = lax.dynamic_slice(value, (0, other), (rows, half))
        return jnp.concatenate([keep, lax.ppermute(send, "seq", CORE_SWAP)], axis=0)

    normed_half = both_cores(normed)
    scaled_half = both_cores(scaled)

    def project(values, weights):
        out = jnp.dot(values, weights, preferred_element_type=f32)
        return out[:rows] + lax.ppermute(out[rows:], "seq", CORE_SWAP)

    gain_q, gain_k = qk_gain[0], qk_gain[1]

    def unit(raw):
        back = lax.rsqrt(jnp.mean(raw * raw, axis=-1, keepdims=True) + 1e-06)
        return raw * back, back

    units = {}
    arrived = {}
    slots = [0] + order
    for step in slots:
        qkv = project(normed_half, w_in[step])
        qh, qs = unit(qkv[:, :dim])
        kh, ks = unit(qkv[:, dim : 2 * dim])
        units[step] = (qh, qs, kh, ks)
        ready = jnp.concatenate([qh * gain_q, kh * gain_k, qkv[:, 2 * dim :]], axis=1).astype(bf16)
        arrived[step] = around(ready, -step, count) if step else ready
    heads = jnp.concatenate([arrived[i] for i in range(count)], axis=0)
    grads = {}
    for step in slots:
        ready = project(scaled_half, w_o[step]).astype(bf16)
        grads[step] = around(ready, -step, count) if step else ready
    g = jnp.concatenate([grads[i] for i in range(count)], axis=0)

    kv = heads[:, dim:]
    kv_chip = lax.ppermute(kv, "seq", CHIP_SWAP)
    kv_all = jnp.concatenate(
        [kv, lax.ppermute(kv, "seq", CORE_SWAP), kv_chip, lax.ppermute(kv_chip, "seq", CORE_SWAP)], axis=0
    )
    dq, dk, dv = attention(heads[:, :dim], g, kv_all[:, :dim], kv_all[:, dim:])
    dkv = jnp.concatenate([dk, dv], axis=1).reshape(4, count * rows, 2 * dim)
    summed = dkv[0::2] + lax.ppermute(dkv[1::2], "seq", CORE_SWAP)
    dkv = summed[0] + lax.ppermute(summed[1].astype(bf16), "seq", CHIP_SWAP).astype(f32)
    back = jnp.concatenate([dq, dkv], axis=1).astype(bf16).reshape(count, rows, 3 * dim)

    def unit_back(hat, scale_back, gain, upstream):
        up = upstream * gain
        return scale_back * (up - hat * jnp.mean(up * hat, axis=-1, keepdims=True))

    grads_in = []
    weights = []
    for step in slots:
        d = around(back[step], step, count) if step else back[0]
        qh, qs, kh, ks = units[step]
        dqn, dkn = d[:, :dim].astype(f32), d[:, dim : 2 * dim].astype(f32)
        grads_in += [
            unit_back(qh, qs, gain_q, dqn).astype(bf16),
            unit_back(kh, ks, gain_k, dkn).astype(bf16),
            d[:, 2 * dim :],
        ]
        weights.append(w_in[step])
    dqkv = jnp.concatenate(grads_in, axis=1)
    dqkv = jnp.concatenate([dqkv, lax.ppermute(dqkv, "seq", CORE_SWAP)], axis=0)
    dn = lax.dot_general(
        dqkv, jnp.concatenate(weights, axis=1), (((1,), (1,)), ((), ())), preferred_element_type=f32
    )
    away = lax.ppermute(dn[rows:].astype(bf16), "seq", CORE_SWAP).astype(f32)
    low = jnp.where(core == 0, dn[:rows], away)
    high = jnp.where(core == 0, away, dn[:rows])
    dhat = jnp.concatenate([low, high], axis=1) * scale
    return cot + inv * (dhat - xhat * jnp.mean(dhat * xhat, axis=-1, keepdims=True))


def solution(mesh):
    placed = (
        P(("group", "seq", "tensor"), None),
        P(("group", "seq", "tensor"), None),
        P("group", None),
        P(None, None, "tensor"),
        P("tensor", None),
        P(),
    )
    sizes = dict(mesh.shape)

    def body(*args):
        weight_elements = args[3].size + args[4].size
        token_elements = 2 * 3 * args[0].size
        if sizes["group"] == 2 and sizes["seq"] == 4 and weight_elements < token_elements:
            return weight_gather_body(sizes["tensor"], *args)
        return token_gather_body(*args)

    return jax.shard_map(
        body,
        mesh=mesh,
        in_specs=placed,
        out_specs=P(("group", "seq", "tensor"), None),
        check_vma=False,
    )
```

```python
import math
from functools import partial

import jax
import jax.numpy as jnp
from jax import lax
from jax.experimental import pallas as pl
from jax.experimental.pallas import tpu as pltpu
from jax.sharding import PartitionSpec as P


def head_norm(raw, gain):
    scale_back = lax.rsqrt(jnp.mean(raw * raw, axis=-1, keepdims=True) + 1e-06)
    return (raw * scale_back * gain, scale_back)


def head_norm_back(raw, scale_back, gain, upstream):
    scaled_up = upstream * gain
    return scale_back * scaled_up - raw * scale_back**3 * jnp.mean(
        raw * scaled_up, axis=-1, keepdims=True
    )


def token_gather_body(tokens, cotangent, modulation, w_qkv, w_out, qk_gain):
    head_dim = qk_gain.shape[1]
    width = w_out.shape[0]
    nheads = width // head_dim
    model_width = tokens.shape[1]
    inv_sqrt = 1.0 / math.sqrt(head_dim)
    modulation_shift = modulation[0]
    modulation_scale = modulation[1]
    gate = modulation[2]
    input_rows_all = tokens.astype(jnp.float32)
    inverse_stddev = lax.rsqrt(
        jnp.mean(input_rows_all * input_rows_all, axis=-1, keepdims=True) + 1e-06
    )
    centered_normalized = input_rows_all * inverse_stddev
    layer_normed = (centered_normalized * (1.0 + modulation_scale) + modulation_shift).astype(
        jnp.bfloat16
    )
    cotangent_rows_all = cotangent.astype(jnp.float32)
    scaled_grad = (cotangent_rows_all * gate).astype(jnp.bfloat16)
    flat_in = w_qkv.reshape(model_width, 3 * width)
    qkv = jnp.dot(
        lax.all_gather(layer_normed, "tensor", axis=0, tiled=True),
        flat_in,
        preferred_element_type=jnp.float32,
    )
    rows = qkv.shape[0]
    query = qkv[:, :width].reshape(rows, nheads, head_dim)
    keys = qkv[:, width : 2 * width].reshape(rows, nheads, head_dim)
    values = qkv[:, 2 * width :].reshape(rows, nheads, head_dim)
    query_n, query_rs = head_norm(query, qk_gain[0])
    keys_n, keys_rs = head_norm(keys, qk_gain[1])
    query_b = query_n.astype(jnp.bfloat16)
    keys_b = keys_n.astype(jnp.bfloat16).reshape(rows, width)
    values_b = values.astype(jnp.bfloat16).reshape(rows, width)
    keys_all, values_all = (
        lax.all_gather(keys_b, "seq", axis=0, tiled=True),
        lax.all_gather(values_b, "seq", axis=0, tiled=True),
    )
    total = keys_all.shape[0]
    block = min(total, 512)
    count_blocks = total // block
    key_stack = keys_all.reshape(count_blocks, block, nheads, head_dim)
    value_stack = values_all.reshape(count_blocks, block, nheads, head_dim)

    def block_scores(queries, block_keys):
        return (
            jnp.einsum("qhd,khd->hqk", queries, block_keys, preferred_element_type=jnp.float32)
            * inv_sqrt
        )

    def stats_step(carry, block_keys):
        row_max, row_sum = carry
        scores = block_scores(query_b, block_keys)
        new_max = jnp.maximum(row_max, jnp.max(scores, axis=-1))
        row_sum = row_sum * jnp.exp(row_max - new_max) + jnp.sum(
            jnp.exp(scores - new_max[..., None]), axis=-1
        )
        return ((new_max, row_sum), None)

    start_max = jnp.full((nheads, rows), -jnp.inf, jnp.float32)
    start_sum = jnp.zeros((nheads, rows), jnp.float32)
    (row_max, row_sum), _ = lax.scan(stats_step, (start_max, start_sum), key_stack)

    def probs_of(scores, bmax, bsum):
        return jnp.exp(scores - bmax[..., None]) / bsum[..., None]

    def output_step(acc, pair):
        weights_b = probs_of(block_scores(query_b, pair[0]), row_max, row_sum).astype(jnp.bfloat16)
        return (
            acc
            + jnp.einsum("hqk,khd->hqd", weights_b, pair[1], preferred_element_type=jnp.float32),
            None,
        )

    attn_acc, _ = lax.scan(
        output_step, jnp.zeros((nheads, rows, head_dim), jnp.float32), (key_stack, value_stack)
    )
    attn_b = attn_acc.astype(jnp.bfloat16)
    dout = lax.dot_general(
        lax.all_gather(scaled_grad, "tensor", axis=0, tiled=True),
        w_out,
        (((1,), (1,)), ((), ())),
        preferred_element_type=jnp.float32,
    )
    grad_b = dout.astype(jnp.bfloat16)
    grad_q = grad_b.reshape(rows, nheads, head_dim)
    delta = jnp.sum(
        jnp.transpose(grad_q, (1, 0, 2)).astype(jnp.float32) * attn_b.astype(jnp.float32), axis=-1
    )

    def grad_terms(queries, grads, block_keys, block_values, bmax, bsum, bdelta):
        weights = probs_of(block_scores(queries, block_keys), bmax, bsum)
        dprob = jnp.einsum("qhd,khd->hqk", grads, block_values, preferred_element_type=jnp.float32)
        dscore = (weights * (dprob - bdelta[..., None])).astype(jnp.bfloat16)
        return (weights.astype(jnp.bfloat16), dscore)

    zeros_heads = jnp.zeros((nheads, rows, head_dim), jnp.float32)

    def both_step(acc, pair):
        weights_b, dscore = grad_terms(query_b, grad_q, pair[0], pair[1], row_max, row_sum, delta)
        acc = (
            acc
            + jnp.einsum("hqk,khd->hqd", dscore, pair[0], preferred_element_type=jnp.float32)
            * inv_sqrt
        )
        dkey_part = (
            jnp.einsum("hqk,qhd->khd", dscore, query_b, preferred_element_type=jnp.float32)
            * inv_sqrt
        )
        dvalue_part = jnp.einsum(
            "hqk,qhd->khd", weights_b, grad_q, preferred_element_type=jnp.float32
        )
        return (
            acc,
            jnp.concatenate(
                [dkey_part.reshape(block, width), dvalue_part.reshape(block, width)], axis=1
            ),
        )

    dquery, key_terms = lax.scan(both_step, zeros_heads, (key_stack, value_stack))
    own_terms = lax.psum_scatter(
        key_terms.reshape(total, 2 * width).astype(jnp.bfloat16),
        "seq",
        scatter_dimension=0,
        tiled=True,
    ).astype(jnp.float32)
    dkey = own_terms[:, :width].reshape(rows, nheads, head_dim)
    dvalue = own_terms[:, width:].reshape(rows, nheads, head_dim)
    dquery = jnp.transpose(dquery, (1, 0, 2))
    dq_raw = head_norm_back(query, query_rs, qk_gain[0], dquery)
    dk_raw = head_norm_back(keys, keys_rs, qk_gain[1], dkey)
    dqkv = jnp.concatenate(
        [dq_raw.reshape(rows, width), dk_raw.reshape(rows, width), dvalue.reshape(rows, width)],
        axis=1,
    ).astype(jnp.bfloat16)
    dnormed = lax.psum_scatter(
        lax.dot_general(
            dqkv, flat_in, (((1,), (1,)), ((), ())), preferred_element_type=jnp.float32
        ).astype(jnp.bfloat16),
        "tensor",
        scatter_dimension=0,
        tiled=True,
    ).astype(jnp.float32)
    normalized_grad = dnormed * (1.0 + modulation_scale)
    final_output = cotangent_rows_all + inverse_stddev * (
        normalized_grad
        - centered_normalized
        * jnp.mean(normalized_grad * centered_normalized, axis=-1, keepdims=True)
    )
    return final_output


CORE_SWAP = [(0, 1), (1, 0), (2, 3), (3, 2)]
CHIP_SWAP = [(0, 2), (2, 0), (1, 3), (3, 1)]
PLANE = ("group", "seq")


def plane_swap(first):
    pairs = []
    for group in range(2):
        for seq in range(4):
            along_chip = (seq % 2 == 0) == first
            to = group * 4 + (seq ^ 2) if along_chip else (1 - group) * 4 + seq
            pairs.append((group * 4 + seq, to))
    return pairs


def around(value, step, count):
    return lax.ppermute(value, "tensor", [(i, (i + step) % count) for i in range(count)])


def attention_kernel(
    scale, block, q_ref, g_ref, k_ref, v_ref, dq_ref, dk_ref, dv_ref, score_ref, prob_ref, dprob_ref
):
    total = k_ref.shape[0]
    rows, dim = q_ref.shape
    steps = total // block
    nt = (((1,), (1,)), ((), ()))
    tn = (((0,), (0,)), ((), ()))

    def scores(i, top):
        here = pl.ds(pl.multiple_of(i * block, block), block)
        s = lax.dot_general(k_ref[here, :], q_ref[...], nt, preferred_element_type=jnp.float32) * scale
        score_ref[here, :] = s
        dprob_ref[here, :] = lax.dot_general(
            v_ref[here, :], g_ref[...], nt, preferred_element_type=jnp.float32
        )
        return jnp.maximum(top, jnp.max(s, axis=0, keepdims=True))

    top = lax.fori_loop(0, steps, scores, jnp.full((1, rows), -jnp.inf, jnp.float32))

    def weigh(i, carry):
        norm, cross = carry
        here = pl.ds(pl.multiple_of(i * block, block), block)
        e = jnp.exp(score_ref[here, :] - top)
        prob_ref[here, :] = e
        return (
            norm + jnp.sum(e, axis=0, keepdims=True),
            cross + jnp.sum(e * dprob_ref[here, :], axis=0, keepdims=True),
        )

    none = jnp.zeros((1, rows), jnp.float32)
    norm, cross = lax.fori_loop(0, steps, weigh, (none, none))
    inverse = 1.0 / norm
    delta = cross * inverse

    def back(i, dq):
        here = pl.ds(pl.multiple_of(i * block, block), block)
        p = prob_ref[here, :] * inverse
        ds = (p * (dprob_ref[here, :] - delta)).astype(jnp.bfloat16)
        dk_ref[here, :] = (
            jnp.dot(ds, q_ref[...], preferred_element_type=jnp.float32) * scale
        )
        dv_ref[here, :] = jnp.dot(
            p.astype(jnp.bfloat16), g_ref[...], preferred_element_type=jnp.float32
        )
        return dq + lax.dot_general(k_ref[here, :], ds, tn, preferred_element_type=jnp.float32)

    dq = lax.fori_loop(0, steps, back, jnp.zeros((dim, rows), jnp.float32))
    dq_ref[...] = dq.T * scale


def attention(q, g, k, v):
    rows, dim = q.shape
    total = k.shape[0]
    f32 = jnp.float32
    vmem = pl.BlockSpec(memory_space=pltpu.VMEM)
    work = rows * total * dim
    return pl.pallas_call(
        partial(attention_kernel, 1.0 / math.sqrt(dim), 256),
        out_shape=(
            jax.ShapeDtypeStruct((rows, dim), f32),
            jax.ShapeDtypeStruct((total, dim), f32),
            jax.ShapeDtypeStruct((total, dim), f32),
        ),
        in_specs=[vmem] * 4,
        out_specs=(vmem,) * 3,
        scratch_shapes=[pltpu.VMEM((total, rows), f32)] * 3,
        compiler_params=pltpu.CompilerParams(vmem_limit_bytes=48 * 1024 * 1024),
        cost_estimate=pl.CostEstimate(
            flops=10 * work, bytes_accessed=16 * total * dim, transcendentals=rows * total
        ),
        name="attention",
    )(q, g, k, v)


def project_kernel(pieces, rows, *refs):
    if pieces:
        places, values = refs[:2]
        blocks = refs[2 : 2 + pieces]
        own_ref, other_ref, whole, sems = refs[2 + pieces :]
        copies = []
        for i, block in enumerate(blocks):
            size = block.shape[0]
            at = pl.ds(pl.multiple_of(places[i] * size, size), size)
            copies.append(pltpu.make_async_copy(block, whole.at[at, :], sems.at[i]))
            copies[-1].start()
        for copy in copies:
            copy.wait()
    else:
        values, whole, own_ref, other_ref = refs
    out = jnp.dot(values[...], whole[...], preferred_element_type=jnp.float32)
    own_ref[...] = out[:rows]
    other_ref[...] = out[rows:]


def project(values, weights, places=None):
    rows = values.shape[0] // 2
    half = values.shape[1]
    f32 = jnp.float32
    pieces = 0 if places is None else len(weights)
    columns = weights[0].shape[1]
    vmem = pl.BlockSpec(memory_space=pltpu.VMEM)
    smem = pl.BlockSpec(memory_space=pltpu.SMEM)
    anywhere = pl.BlockSpec(memory_space=pl.ANY)
    scratch = [pltpu.VMEM((half, columns), jnp.bfloat16), pltpu.SemaphoreType.DMA((pieces,))]
    return pl.pallas_call(
        partial(project_kernel, pieces, rows),
        out_shape=(jax.ShapeDtypeStruct((rows, columns), f32),) * 2,
        in_specs=[smem, vmem] + [anywhere] * pieces if pieces else [vmem, vmem],
        out_specs=(vmem, vmem),
        scratch_shapes=scratch if pieces else [],
        compiler_params=pltpu.CompilerParams(vmem_limit_bytes=32 * 1024 * 1024),
        cost_estimate=pl.CostEstimate(
            flops=4 * rows * half * columns,
            bytes_accessed=2 * half * (columns + 2 * rows),
            transcendentals=0,
        ),
        name="project",
    )(*((places,) if pieces else ()), values, *weights)


def unit(raw):
    back = lax.rsqrt(jnp.mean(raw * raw, axis=-1, keepdims=True) + 1e-06)
    return raw * back, back


def finish_kernel(own_ref, come_ref, gain_ref, raw_ref, query_ref, kv_ref):
    raw = own_ref[...] + come_ref[...]
    raw_ref[...] = raw
    dim = query_ref.shape[1]
    qh, _ = unit(raw[:, :dim])
    kh, _ = unit(raw[:, dim : 2 * dim])
    query_ref[...] = (qh * gain_ref[0:1, :]).astype(jnp.bfloat16)
    kv_ref[:, :dim] = (kh * gain_ref[1:2, :]).astype(jnp.bfloat16)
    kv_ref[:, dim:] = raw[:, 2 * dim :].astype(jnp.bfloat16)


def finish(own, come, gains):
    rows, dim = own.shape[0], gains.shape[1]
    vmem = pl.BlockSpec(memory_space=pltpu.VMEM)
    return pl.pallas_call(
        finish_kernel,
        out_shape=(
            jax.ShapeDtypeStruct(own.shape, jnp.float32),
            jax.ShapeDtypeStruct((rows, dim), jnp.bfloat16),
            jax.ShapeDtypeStruct((rows, 2 * dim), jnp.bfloat16),
        ),
        in_specs=[vmem] * 3,
        out_specs=(vmem,) * 3,
        cost_estimate=pl.CostEstimate(
            flops=20 * own.size, bytes_accessed=16 * own.size, transcendentals=2 * rows
        ),
        name="finish",
    )(own, come, gains)


def unfinish_kernel(count, gain_ref, *refs):
    raws, dqs, dkvs, out_ref = refs[:count], refs[count : 2 * count], refs[2 * count : 3 * count], refs[-1]
    dim = gain_ref.shape[1]

    def unit_back(raw, gain, upstream):
        hat, scale_back = unit(raw)
        up = upstream.astype(jnp.float32) * gain
        return scale_back * (up - hat * jnp.mean(up * hat, axis=-1, keepdims=True))

    for i in range(count):
        at = 3 * dim * i
        raw, dkv = raws[i], dkvs[i]
        dq = unit_back(raw[:, :dim], gain_ref[0:1, :], dqs[i][...])
        dk = unit_back(raw[:, dim : 2 * dim], gain_ref[1:2, :], dkv[:, :dim])
        out_ref[:, at : at + dim] = dq.astype(jnp.bfloat16)
        out_ref[:, at + dim : at + 2 * dim] = dk.astype(jnp.bfloat16)
        out_ref[:, at + 2 * dim : at + 3 * dim] = dkv[:, dim:]


def unfinish(gains, raws, dqs, dkvs):
    count = len(raws)
    rows, columns = raws[0].shape
    vmem = pl.BlockSpec(memory_space=pltpu.VMEM)
    return pl.pallas_call(
        partial(unfinish_kernel, count),
        out_shape=jax.ShapeDtypeStruct((rows, count * columns), jnp.bfloat16),
        in_specs=[vmem] * (1 + 3 * count),
        out_specs=vmem,
        cost_estimate=pl.CostEstimate(
            flops=20 * count * rows * columns,
            bytes_accessed=8 * count * rows * columns,
            transcendentals=2 * rows,
        ),
        name="unfinish",
    )(gains, *raws, *dqs, *dkvs)


def back_project_kernel(count, places, mine, theirs, *refs):
    whole_own = refs[0]
    blocks = [refs[1 + 4 * i : 5 + 4 * i] for i in range(count - 1)]
    own_ref, other_ref, grads, whole, sems = refs[1 + 4 * (count - 1) :]
    rows, columns = mine.shape
    part = blocks[0][0].shape[0]
    width = columns // count
    copies = []
    for i, four in enumerate(blocks):
        copies.append([])
        for j, block in enumerate(four):
            at = pl.ds(pl.multiple_of(places[j] * part, part), part)
            copies[i].append(pltpu.make_async_copy(block, whole.at[i, at, :], sems.at[4 * i + j]))
            copies[i][j].start()
    grads[:rows] = mine[...]
    grads[rows:] = theirs[...]
    nt = (((1,), (1,)), ((), ()))
    total = lax.dot_general(grads[:, :width], whole_own[...], nt, preferred_element_type=jnp.float32)
    for i, four in enumerate(copies):
        for copy in four:
            copy.wait()
        at = width * (i + 1)
        total += lax.dot_general(
            grads[:, at : at + width], whole[i], nt, preferred_element_type=jnp.float32
        )
    own_ref[...] = total[:rows]
    other_ref[...] = total[rows:].astype(jnp.bfloat16)


def back_project(mine, theirs, whole_own, blocks, places):
    count = 1 + len(blocks)
    rows, columns = mine.shape
    half, width = whole_own.shape
    vmem = pl.BlockSpec(memory_space=pltpu.VMEM)
    smem = pl.BlockSpec(memory_space=pltpu.SMEM)
    anywhere = pl.BlockSpec(memory_space=pl.ANY)
    flat = [block for four in blocks for block in four]
    return pl.pallas_call(
        partial(back_project_kernel, count),
        out_shape=(
            jax.ShapeDtypeStruct((rows, half), jnp.float32),
            jax.ShapeDtypeStruct((rows, half), jnp.bfloat16),
        ),
        in_specs=[smem, vmem, vmem, vmem] + [anywhere] * len(flat),
        out_specs=(vmem, vmem),
        scratch_shapes=[
            pltpu.VMEM((2 * rows, columns), jnp.bfloat16),
            pltpu.VMEM((count - 1, half, width), jnp.bfloat16),
            pltpu.SemaphoreType.DMA((len(flat),)),
        ],
        compiler_params=pltpu.CompilerParams(vmem_limit_bytes=40 * 1024 * 1024),
        cost_estimate=pl.CostEstimate(
            flops=4 * rows * half * columns, bytes_accessed=2 * half * columns, transcendentals=0
        ),
        name="back_project",
    )(places, mine, theirs, whole_own, *flat)


def after(value, *earlier):
    return lax.optimization_barrier((value, *earlier))[0]


def weight_gather_body(count, tokens, cotangent, modulation, w_qkv, w_out, qk_gain):
    bf16, f32 = jnp.bfloat16, jnp.float32
    dim = qk_gain.shape[1]
    rows, width = tokens.shape
    half = width // 2
    part = half // 4
    seq = lax.axis_index("seq")
    core, chip, group = seq % 2, seq // 2, lax.axis_index("group")
    this = core * half
    other = half - this
    mine = 2 * group + chip
    across = 2 * group + (1 - chip)
    over = 2 * (1 - group) + chip
    far = 3 - mine
    places = jnp.stack(
        [mine, jnp.where(core == 0, across, over), jnp.where(core == 0, over, across), far]
    ).astype(jnp.int32)
    side = jnp.where(core == 0, chip, group)
    sides = jnp.stack([side, 1 - side]).astype(jnp.int32)

    def hand_round(own):
        one = lax.ppermute(own, PLANE, plane_swap(True))
        two = lax.ppermute(own, PLANE, plane_swap(False))
        return own, one, two, lax.ppermute(one, PLANE, plane_swap(False))

    order = [1, count - 1] + list(range(2, count - 1))
    own_in = lax.dynamic_slice(w_qkv, (this + mine * part, 0, 0), (part, 3, dim)).reshape(part, 3 * dim)
    w_in, w_o = {}, {}
    last = None
    for step in order:
        last = around(own_in if last is None else after(own_in, last), step, count)
        w_in[step] = hand_round(last)
    own_out = lax.dynamic_slice(w_out, (0, this + side * 2 * part), (dim, 2 * part)).T
    for step in order:
        last = around(after(own_out, last), step, count)
        w_o[step] = (last, lax.ppermute(last, PLANE, plane_swap(True)))

    shift, scale, gate = modulation[0], 1.0 + modulation[1], modulation[2]
    x = tokens.astype(f32)
    inv = lax.rsqrt(jnp.mean(x * x, axis=-1, keepdims=True) + 1e-06)
    xhat = x * inv
    normed = (xhat * scale + shift).astype(bf16)
    cot = cotangent.astype(f32)
    scaled = (cot * gate).astype(bf16)

    def both_cores(value):
        keep = lax.dynamic_slice(value, (0, this), (rows, half))
        send = lax.dynamic_slice(value, (0, other), (rows, half))
        return jnp.concatenate([keep, lax.ppermute(send, "seq", CORE_SWAP)], axis=0)

    normed_half = both_cores(normed)
    scaled_half = both_cores(scaled)
    w_in_half = lax.dynamic_slice(w_qkv, (this, 0, 0), (half, 3, dim)).reshape(half, 3 * dim)
    w_out_half = lax.dynamic_slice(w_out, (0, this), (dim, half)).T

    slots = [0] + order
    raws, queries, kvs, grads = {}, {}, {}, {}
    for step in slots:
        if step:
            own, away = project(normed_half, w_in[step], places)
        else:
            own, away = project(normed_half, (w_in_half,))
        raw, query, kv = finish(own, lax.ppermute(away, "seq", CORE_SWAP), qk_gain)
        raws[step] = raw
        queries[step] = around(query, -step, count) if step else query
        kvs[step] = around(kv, -step, count) if step else kv
    for step in slots:
        if step:
            own, away = project(scaled_half, w_o[step], sides)
        else:
            own, away = project(scaled_half, (w_out_half,))
        ready = (own + lax.ppermute(away, "seq", CORE_SWAP)).astype(bf16)
        grads[step] = around(ready, -step, count) if step else ready
    q = jnp.concatenate([queries[i] for i in slots], axis=0)
    g = jnp.concatenate([grads[i] for i in slots], axis=0)
    kv = jnp.concatenate([kvs[i] for i in slots], axis=0)

    kv_chip = lax.ppermute(kv, "seq", CHIP_SWAP)
    kv_all = jnp.concatenate(
        [kv, lax.ppermute(kv, "seq", CORE_SWAP), kv_chip, lax.ppermute(kv_chip, "seq", CORE_SWAP)], axis=0
    )
    dq, dk, dv = attention(q, g, kv_all[:, :dim], kv_all[:, dim:])
    dq = dq.astype(bf16).reshape(count, rows, dim)
    dqs = {step: around(dq[i], step, count) if step else dq[i] for i, step in enumerate(slots)}
    dkv = jnp.concatenate([dk, dv], axis=1).reshape(4, count * rows, 2 * dim)
    summed = dkv[0::2] + lax.ppermute(dkv[1::2], "seq", CORE_SWAP)
    dkv = summed[0] + lax.ppermute(summed[1].astype(bf16), "seq", CHIP_SWAP).astype(f32)
    dkv = dkv.astype(bf16).reshape(count, rows, 2 * dim)
    dkvs = {step: around(dkv[i], step, count) if step else dkv[i] for i, step in enumerate(slots)}

    dqkv = unfinish(qk_gain, *[[each[i] for i in slots] for each in (raws, dqs, dkvs)])
    own, away = back_project(
        dqkv, lax.ppermute(dqkv, "seq", CORE_SWAP), w_in_half, [w_in[i] for i in order], places
    )
    away = lax.ppermute(away, "seq", CORE_SWAP).astype(f32)
    low = jnp.where(core == 0, own, away)
    high = jnp.where(core == 0, away, own)
    dhat = jnp.concatenate([low, high], axis=1) * scale
    return cot + inv * (dhat - xhat * jnp.mean(dhat * xhat, axis=-1, keepdims=True))


def solution(mesh):
    placed = (
        P(("group", "seq", "tensor"), None),
        P(("group", "seq", "tensor"), None),
        P("group", None),
        P(None, None, "tensor"),
        P("tensor", None),
        P(),
    )
    sizes = dict(mesh.shape)

    def body(*args):
        weight_elements = args[3].size + args[4].size
        token_elements = 2 * 3 * args[0].size
        if sizes["group"] == 2 and sizes["seq"] == 4 and weight_elements < token_elements:
            return weight_gather_body(sizes["tensor"], *args)
        return token_gather_body(*args)

    return jax.shard_map(
        body,
        mesh=mesh,
        in_specs=placed,
        out_specs=P(("group", "seq", "tensor"), None),
        check_vma=False,
    )
```

```python
import math
from functools import partial

import jax
import jax.numpy as jnp
from jax import lax
from jax.experimental import pallas as pl
from jax.experimental.pallas import tpu as pltpu
from jax.sharding import PartitionSpec as P


def head_norm(raw, gain):
    scale_back = lax.rsqrt(jnp.mean(raw * raw, axis=-1, keepdims=True) + 1e-06)
    return (raw * scale_back * gain, scale_back)


def head_norm_back(raw, scale_back, gain, upstream):
    scaled_up = upstream * gain
    return scale_back * scaled_up - raw * scale_back**3 * jnp.mean(
        raw * scaled_up, axis=-1, keepdims=True
    )


def token_gather_body(tokens, cotangent, modulation, w_qkv, w_out, qk_gain):
    head_dim = qk_gain.shape[1]
    width = w_out.shape[0]
    nheads = width // head_dim
    model_width = tokens.shape[1]
    inv_sqrt = 1.0 / math.sqrt(head_dim)
    modulation_shift = modulation[0]
    modulation_scale = modulation[1]
    gate = modulation[2]
    input_rows_all = tokens.astype(jnp.float32)
    inverse_stddev = lax.rsqrt(
        jnp.mean(input_rows_all * input_rows_all, axis=-1, keepdims=True) + 1e-06
    )
    centered_normalized = input_rows_all * inverse_stddev
    layer_normed = (centered_normalized * (1.0 + modulation_scale) + modulation_shift).astype(
        jnp.bfloat16
    )
    cotangent_rows_all = cotangent.astype(jnp.float32)
    scaled_grad = (cotangent_rows_all * gate).astype(jnp.bfloat16)
    flat_in = w_qkv.reshape(model_width, 3 * width)
    qkv = jnp.dot(
        lax.all_gather(layer_normed, "tensor", axis=0, tiled=True),
        flat_in,
        preferred_element_type=jnp.float32,
    )
    rows = qkv.shape[0]
    query = qkv[:, :width].reshape(rows, nheads, head_dim)
    keys = qkv[:, width : 2 * width].reshape(rows, nheads, head_dim)
    values = qkv[:, 2 * width :].reshape(rows, nheads, head_dim)
    query_n, query_rs = head_norm(query, qk_gain[0])
    keys_n, keys_rs = head_norm(keys, qk_gain[1])
    query_b = query_n.astype(jnp.bfloat16)
    keys_b = keys_n.astype(jnp.bfloat16).reshape(rows, width)
    values_b = values.astype(jnp.bfloat16).reshape(rows, width)
    keys_all, values_all = (
        lax.all_gather(keys_b, "seq", axis=0, tiled=True),
        lax.all_gather(values_b, "seq", axis=0, tiled=True),
    )
    total = keys_all.shape[0]
    block = min(total, 512)
    count_blocks = total // block
    key_stack = keys_all.reshape(count_blocks, block, nheads, head_dim)
    value_stack = values_all.reshape(count_blocks, block, nheads, head_dim)

    def block_scores(queries, block_keys):
        return (
            jnp.einsum("qhd,khd->hqk", queries, block_keys, preferred_element_type=jnp.float32)
            * inv_sqrt
        )

    def stats_step(carry, block_keys):
        row_max, row_sum = carry
        scores = block_scores(query_b, block_keys)
        new_max = jnp.maximum(row_max, jnp.max(scores, axis=-1))
        row_sum = row_sum * jnp.exp(row_max - new_max) + jnp.sum(
            jnp.exp(scores - new_max[..., None]), axis=-1
        )
        return ((new_max, row_sum), None)

    start_max = jnp.full((nheads, rows), -jnp.inf, jnp.float32)
    start_sum = jnp.zeros((nheads, rows), jnp.float32)
    (row_max, row_sum), _ = lax.scan(stats_step, (start_max, start_sum), key_stack)

    def probs_of(scores, bmax, bsum):
        return jnp.exp(scores - bmax[..., None]) / bsum[..., None]

    def output_step(acc, pair):
        weights_b = probs_of(block_scores(query_b, pair[0]), row_max, row_sum).astype(jnp.bfloat16)
        return (
            acc
            + jnp.einsum("hqk,khd->hqd", weights_b, pair[1], preferred_element_type=jnp.float32),
            None,
        )

    attn_acc, _ = lax.scan(
        output_step, jnp.zeros((nheads, rows, head_dim), jnp.float32), (key_stack, value_stack)
    )
    attn_b = attn_acc.astype(jnp.bfloat16)
    dout = lax.dot_general(
        lax.all_gather(scaled_grad, "tensor", axis=0, tiled=True),
        w_out,
        (((1,), (1,)), ((), ())),
        preferred_element_type=jnp.float32,
    )
    grad_b = dout.astype(jnp.bfloat16)
    grad_q = grad_b.reshape(rows, nheads, head_dim)
    delta = jnp.sum(
        jnp.transpose(grad_q, (1, 0, 2)).astype(jnp.float32) * attn_b.astype(jnp.float32), axis=-1
    )

    def grad_terms(queries, grads, block_keys, block_values, bmax, bsum, bdelta):
        weights = probs_of(block_scores(queries, block_keys), bmax, bsum)
        dprob = jnp.einsum("qhd,khd->hqk", grads, block_values, preferred_element_type=jnp.float32)
        dscore = (weights * (dprob - bdelta[..., None])).astype(jnp.bfloat16)
        return (weights.astype(jnp.bfloat16), dscore)

    zeros_heads = jnp.zeros((nheads, rows, head_dim), jnp.float32)

    def both_step(acc, pair):
        weights_b, dscore = grad_terms(query_b, grad_q, pair[0], pair[1], row_max, row_sum, delta)
        acc = (
            acc
            + jnp.einsum("hqk,khd->hqd", dscore, pair[0], preferred_element_type=jnp.float32)
            * inv_sqrt
        )
        dkey_part = (
            jnp.einsum("hqk,qhd->khd", dscore, query_b, preferred_element_type=jnp.float32)
            * inv_sqrt
        )
        dvalue_part = jnp.einsum(
            "hqk,qhd->khd", weights_b, grad_q, preferred_element_type=jnp.float32
        )
        return (
            acc,
            jnp.concatenate(
                [dkey_part.reshape(block, width), dvalue_part.reshape(block, width)], axis=1
            ),
        )

    dquery, key_terms = lax.scan(both_step, zeros_heads, (key_stack, value_stack))
    own_terms = lax.psum_scatter(
        key_terms.reshape(total, 2 * width).astype(jnp.bfloat16),
        "seq",
        scatter_dimension=0,
        tiled=True,
    ).astype(jnp.float32)
    dkey = own_terms[:, :width].reshape(rows, nheads, head_dim)
    dvalue = own_terms[:, width:].reshape(rows, nheads, head_dim)
    dquery = jnp.transpose(dquery, (1, 0, 2))
    dq_raw = head_norm_back(query, query_rs, qk_gain[0], dquery)
    dk_raw = head_norm_back(keys, keys_rs, qk_gain[1], dkey)
    dqkv = jnp.concatenate(
        [dq_raw.reshape(rows, width), dk_raw.reshape(rows, width), dvalue.reshape(rows, width)],
        axis=1,
    ).astype(jnp.bfloat16)
    dnormed = lax.psum_scatter(
        lax.dot_general(
            dqkv, flat_in, (((1,), (1,)), ((), ())), preferred_element_type=jnp.float32
        ).astype(jnp.bfloat16),
        "tensor",
        scatter_dimension=0,
        tiled=True,
    ).astype(jnp.float32)
    normalized_grad = dnormed * (1.0 + modulation_scale)
    final_output = cotangent_rows_all + inverse_stddev * (
        normalized_grad
        - centered_normalized
        * jnp.mean(normalized_grad * centered_normalized, axis=-1, keepdims=True)
    )
    return final_output


CORE_SWAP = [(0, 1), (1, 0), (2, 3), (3, 2)]
CHIP_SWAP = [(0, 2), (2, 0), (1, 3), (3, 1)]
PLANE = ("group", "seq")


def plane_swap(first):
    pairs = []
    for group in range(2):
        for seq in range(4):
            along_chip = (seq % 2 == 0) == first
            to = group * 4 + (seq ^ 2) if along_chip else (1 - group) * 4 + seq
            pairs.append((group * 4 + seq, to))
    return pairs


def around(value, step, count):
    return lax.ppermute(value, "tensor", [(i, (i + step) % count) for i in range(count)])


def place():
    seq = lax.axis_index("seq")
    core, chip, group = seq & 1, seq >> 1, lax.axis_index("group")
    return core, chip, group, 2 * group + chip


def arrivals():
    core, chip, group, mine = place()
    across = 2 * group + (1 - chip)
    over = 2 * (1 - group) + chip
    return mine, jnp.where(core == 0, across, over), jnp.where(core == 0, over, across), 3 - mine


def call(kernel, name, out, operands, megabytes, flops=0, touched=0, roots=0, far=(), scratch=()):
    vmem = pl.BlockSpec(memory_space=pltpu.VMEM)
    anywhere = pl.BlockSpec(memory_space=pl.ANY)
    out = tuple(jax.ShapeDtypeStruct(shape, dtype) for shape, dtype in out)
    return pl.pallas_call(
        kernel,
        out_shape=out,
        in_specs=[anywhere if i in far else vmem for i in range(len(operands))],
        out_specs=(vmem,) * len(out),
        scratch_shapes=list(scratch),
        compiler_params=pltpu.CompilerParams(vmem_limit_bytes=megabytes and megabytes * 1024 * 1024),
        cost_estimate=pl.CostEstimate(flops=0, bytes_accessed=0, transcendentals=0),
        name=name,
    )(*operands)


BF16, F32 = jnp.bfloat16, jnp.float32
NT = (((1,), (1,)), ((), ()))
TN = (((0,), (0,)), ((), ()))


def pack_kernel(w_in, w_out, early, late, quarter, sems):
    core, _, _, mine = place()
    part, dim = early.shape[1:]
    half, tile = 4 * part, dim // 4
    rows = pl.ds(pl.multiple_of(core * half + mine * part, tile), part)
    targets = (early.at[0], early.at[1], late.at[0])
    copies = [pltpu.make_async_copy(w_in.at[j, rows, :], to, sems.at[j]) for j, to in enumerate(targets)]
    lanes = pl.ds(pl.multiple_of(core * half, dim), half)
    heads = pl.ds(pl.multiple_of(mine * tile, tile), tile)
    copies.append(pltpu.make_async_copy(w_out.at[heads, lanes], quarter, sems.at[3]))
    for copy in copies:
        copy.start()
    for copy in copies:
        copy.wait()
    for i in range(part // tile):
        late[1, i * tile : (i + 1) * tile, :] = quarter[:, i * dim : (i + 1) * dim]


def pack(w_in, w_out):
    _, width, dim = w_in.shape
    part = width // 8
    return call(
        pack_kernel,
        "pack",
        [((2, part, dim), BF16)] * 2,
        (w_in, w_out),
        None,
        touched=16 * part * dim,
        far=(0, 1),
        scratch=[pltpu.VMEM((dim // 4, 4 * part), BF16), pltpu.SemaphoreType.DMA((4,))],
    )


def front_kernel(x_ref, c_ref, mod_ref, keep_ref, send_ref, inv_ref):
    half = keep_ref.shape[1] // 2
    core = place()[0]
    x = x_ref[...].astype(F32)
    inv = lax.rsqrt(jnp.mean(x * x, axis=-1, keepdims=True) + 1e-06)
    inv_ref[...] = inv
    for i in range(2):
        at = pl.ds(i * half, half)
        xhat = x_ref[:, at].astype(F32) * inv
        normed = (xhat * (1.0 + mod_ref[1:2, at]) + mod_ref[0:1, at]).astype(BF16)
        scaled = (c_ref[:, at].astype(F32) * mod_ref[2:3, at]).astype(BF16)

        @pl.when(core == i)
        def _():
            keep_ref[:, :half] = normed
            keep_ref[:, half:] = scaled

        @pl.when(core != i)
        def _():
            send_ref[:, :half] = normed
            send_ref[:, half:] = scaled


def front(tokens, cotangent, modulation):
    size = tokens.size
    return call(
        front_kernel,
        "front",
        [(tokens.shape, BF16), (tokens.shape, BF16), ((tokens.shape[0], 1), F32)],
        (tokens, cotangent, modulation),
        12,
        flops=20 * size,
        touched=8 * size,
    )


def project_kernel(first, keep_ref, come_ref, *refs):
    rows, half = keep_ref.shape[0], keep_ref.shape[1] // 2
    if first:
        w_in, w_out, own_ref, away_ref, whole, whole_out, sems = refs
        dim = w_in.shape[2]
        at = pl.ds(pl.multiple_of(place()[0] * half, dim), half)
        copies = [
            pltpu.make_async_copy(w_in.at[j, at, :], whole.at[:, j * dim : (j + 1) * dim], sems.at[j])
            for j in range(3)
        ]
        copies.append(pltpu.make_async_copy(w_out.at[:, at], whole_out, sems.at[3]))
        for copy in copies:
            copy.start()
        for copy in copies:
            copy.wait()
    else:
        *blocks, own_ref, away_ref, whole, whole_out = refs
        dim = whole_out.shape[0]
        tile = dim // 4
        for early, late, at in zip(blocks[:4], blocks[4:], arrivals()):
            part = early.shape[1]
            to = pl.ds(pl.multiple_of(at * part, tile), part)
            for j, block in enumerate((early[0], early[1], late[0])):
                whole[to, j * dim : (j + 1) * dim] = block
            to = pl.ds(pl.multiple_of(at * tile, tile), tile)
            for t in range(part // tile):
                whole_out[to, t * dim : (t + 1) * dim] = late[1, t * tile : (t + 1) * tile, :]
    x = jnp.concatenate([keep_ref[...], come_ref[...]], axis=0)
    qkv = jnp.dot(x[:, :half], whole[...], preferred_element_type=F32)
    grad = lax.dot_general(x[:, half:], whole_out[...], NT, preferred_element_type=F32)
    own_ref[:, : 3 * dim] = qkv[:rows]
    own_ref[:, 3 * dim :] = grad[:rows]
    away_ref[:, : 3 * dim] = qkv[rows:]
    away_ref[:, 3 * dim :] = grad[rows:]


def project(keep, come, blocks, weights=()):
    rows, half = keep.shape[0], keep.shape[1] // 2
    first = len(weights) == 2
    dim = weights[0].shape[2] if first else blocks[0][0].shape[2]
    sums = ((rows, 4 * dim), F32)
    return call(
        partial(project_kernel, first),
        "project",
        [sums, sums, ((half, 3 * dim), BF16)],
        (keep, come, *weights, *[block for eight in blocks for block in eight]),
        12,
        flops=16 * rows * half * dim,
        touched=8 * half * (dim + rows),
        far=(2, 3) if first else (),
        scratch=[pltpu.VMEM((dim, half), BF16)] + [pltpu.SemaphoreType.DMA((4,))] * first,
    )


def unit(raw):
    back = lax.rsqrt(jnp.mean(raw * raw, axis=-1, keepdims=True) + 1e-06)
    return raw * back, back


def finish_kernel(slots, own_ref, come_ref, gain_ref, raw_ref, *refs):
    dim = gain_ref.shape[1]
    for i in range(slots):
        at = 4 * dim * i
        raw = own_ref[:, at : at + 4 * dim] + come_ref[:, at : at + 4 * dim]
        raw_ref[:, 2 * dim * i : 2 * dim * (i + 1)] = raw[:, : 2 * dim]
        qh, _ = unit(raw[:, :dim])
        kh, _ = unit(raw[:, dim : 2 * dim])
        kv_ref, qg_ref = refs[i], refs[slots + i]
        qg_ref[:, :dim] = (qh * gain_ref[0:1, :]).astype(BF16)
        qg_ref[:, dim:] = raw[:, 3 * dim :].astype(BF16)
        kv_ref[:, :dim] = (kh * gain_ref[1:2, :]).astype(BF16)
        kv_ref[:, dim:] = raw[:, 2 * dim : 3 * dim].astype(BF16)


def finish(own, come, gains):
    rows, dim = own.shape[0], gains.shape[1]
    slots = own.shape[1] // (4 * dim)
    raw, *refs = call(
        partial(finish_kernel, slots),
        "finish",
        [((rows, 2 * dim * slots), F32)] + [((rows, 2 * dim), BF16)] * (2 * slots),
        (own, come, gains),
        6,
        flops=20 * own.size,
        touched=16 * own.size,
        roots=2 * rows * slots,
    )
    return raw, refs[:slots], refs[slots:]


def attention_kernel(scale, block, slots, *refs):
    qgs, kvs = refs[:slots], refs[slots:-9]
    dq_ref, stay_ref, send_ref, q_ref, g_ref, k_ref, v_ref, prob_ref, dprob_ref = refs[-9:]
    total, dim = k_ref.shape
    rows = q_ref.shape[0]
    steps = total // block
    for i, qg in enumerate(qgs):
        at = pl.ds(i * qg.shape[0], qg.shape[0])
        q_ref[at, :] = qg[:, :dim]
        g_ref[at, :] = qg[:, dim:]
    at = 0
    for kv in kvs:
        k_ref[pl.ds(at, kv.shape[0]), :] = kv[:, :dim]
        v_ref[pl.ds(at, kv.shape[0]), :] = kv[:, dim:]
        at += kv.shape[0]

    def scores(i, top):
        here = pl.ds(pl.multiple_of(i * block, block), block)
        s = lax.dot_general(k_ref[here, :], q_ref[...], NT, preferred_element_type=F32) * scale
        prob_ref[here, :] = s
        dprob_ref[here, :] = lax.dot_general(
            v_ref[here, :], g_ref[...], NT, preferred_element_type=F32
        )
        return jnp.maximum(top, jnp.max(s, axis=0, keepdims=True))

    top = lax.fori_loop(0, steps, scores, jnp.full((1, rows), -jnp.inf, F32))

    def weigh(i, carry):
        norm, cross = carry
        here = pl.ds(pl.multiple_of(i * block, block), block)
        e = jnp.exp(prob_ref[here, :] - top)
        prob_ref[here, :] = e
        return (
            norm + jnp.sum(e, axis=0, keepdims=True),
            cross + jnp.sum(e * dprob_ref[here, :], axis=0, keepdims=True),
        )

    none = jnp.zeros((1, rows), F32)
    norm, cross = lax.fori_loop(0, steps, weigh, (none, none))
    inverse = 1.0 / norm
    delta = cross * inverse
    dq = jnp.zeros((dim, rows), F32)
    quarter = total // 4
    for turn in range(4):
        out_ref = (stay_ref, send_ref)[turn % 2]

        def back(i, dq):
            here = pl.ds(pl.multiple_of(turn * quarter + i * block, block), block)
            to = pl.ds(pl.multiple_of(i * block, block), block)
            p = prob_ref[here, :] * inverse
            ds = (p * (dprob_ref[here, :] - delta)).astype(BF16)
            out_ref[turn // 2, to, :dim] = jnp.dot(ds, q_ref[...], preferred_element_type=F32) * scale
            out_ref[turn // 2, to, dim:] = jnp.dot(
                p.astype(BF16), g_ref[...], preferred_element_type=F32
            )
            return dq + lax.dot_general(k_ref[here, :], ds, TN, preferred_element_type=F32)

        dq = lax.fori_loop(0, quarter // block, back, dq)
    dq_ref[...] = (dq.T * scale).astype(BF16)


def attention(qgs, kvs):
    dim = qgs[0].shape[1] // 2
    rows = sum(qg.shape[0] for qg in qgs)
    total = 4 * rows
    work = rows * total * dim
    block = rows // 2
    terms = ((2, rows, 2 * dim), F32)
    return call(
        partial(attention_kernel, 1.0 / math.sqrt(dim), block, len(qgs)),
        "attention",
        [((rows, dim), BF16), terms, terms],
        (*qgs, *kvs),
        24,
        flops=10 * work,
        touched=16 * total * dim,
        roots=rows * total,
        scratch=[pltpu.VMEM((rows, dim), BF16)] * 2
        + [pltpu.VMEM((total, dim), BF16)] * 2
        + [pltpu.VMEM((total, rows), F32)] * 2,
    )


def unfinish_kernel(slots, gain_ref, *refs):
    raws, dqs, dkvs = refs[:slots], refs[slots : 2 * slots], refs[2 * slots : 3 * slots]
    out_ref = refs[-1]
    dim = gain_ref.shape[1]

    def unit_back(raw, gain, upstream):
        hat, scale_back = unit(raw)
        up = upstream.astype(F32) * gain
        return scale_back * (up - hat * jnp.mean(up * hat, axis=-1, keepdims=True))

    for i, (raw, dq, dkv) in enumerate(zip(raws, dqs, dkvs)):
        at = 3 * dim * i
        dq = unit_back(raw[:, :dim], gain_ref[0:1, :], dq[...])
        dk = unit_back(raw[:, dim:], gain_ref[1:2, :], dkv[:, :dim])
        out_ref[:, at : at + dim] = dq.astype(BF16)
        out_ref[:, at + dim : at + 2 * dim] = dk.astype(BF16)
        out_ref[:, at + 2 * dim : at + 3 * dim] = dkv[:, dim:]


def unfinish(gains, raws, dqs, dkvs):
    slots, (rows, dim) = len(dqs), dqs[0].shape
    return call(
        partial(unfinish_kernel, slots),
        "unfinish",
        [((rows, 3 * dim * slots), BF16)],
        (gains, *raws, *dqs, *dkvs),
        6,
        flops=60 * slots * rows * dim,
        touched=24 * slots * rows * dim,
        roots=2 * rows * slots,
    )[0]


def back_project_kernel(mine, theirs, *refs):
    weights, (own_ref, away_ref) = refs[:-2], refs[-2:]
    rows, half = own_ref.shape
    width = mine.shape[1] // len(weights)
    grads = jnp.concatenate([mine[...], theirs[...]], axis=0)
    step = half // 7 if half % 7 == 0 else half
    for to in range(0, half, step):
        total = None
        for i, whole in enumerate(weights):
            part = lax.dot_general(
                grads[:, width * i : width * (i + 1)],
                whole[to : to + step, :],
                NT,
                preferred_element_type=F32,
            )
            total = part if total is None else total + part
        own_ref[:, to : to + step] = total[:rows]
        away_ref[:, to : to + step] = total[rows:].astype(BF16)


def back_project(mine, theirs, weights):
    (rows, columns), half = mine.shape, weights[0].shape[0]
    return call(
        back_project_kernel,
        "back_project",
        [((rows, half), F32), ((rows, half), BF16)],
        (mine, theirs, *weights),
        16,
        flops=4 * rows * half * columns,
        touched=2 * half * columns,
    )


def close_kernel(own_ref, away_ref, x_ref, c_ref, mod_ref, inv_ref, out_ref):
    half = own_ref.shape[1]
    core = place()[0]
    inv = inv_ref[...]
    total = 0.0
    for i in range(2):
        at = pl.ds(i * half, half)
        grad = jnp.where(core == i, own_ref[...], away_ref[...].astype(F32))
        dhat = grad * (1.0 + mod_ref[1:2, at])
        out_ref[:, at] = dhat
        total += jnp.sum(dhat * x_ref[:, at].astype(F32), axis=-1, keepdims=True)
    cross = total * (inv * inv * (0.5 / half))
    for i in range(2):
        at = pl.ds(i * half, half)
        dhat = out_ref[:, at] - x_ref[:, at].astype(F32) * cross
        out_ref[:, at] = c_ref[:, at].astype(F32) + inv * dhat


def close(own, away, tokens, cotangent, modulation, inv):
    size = tokens.size
    return call(
        close_kernel,
        "close",
        [(tokens.shape, F32)],
        (own, away, tokens, cotangent, modulation, inv),
        12,
        flops=10 * size,
        touched=12 * size,
    )[0]


def after(value, *earlier):
    return lax.optimization_barrier((value, *earlier))[0]


def weight_gather_body(count, tokens, cotangent, modulation, w_qkv, w_out, qk_gain):
    rows, dim = tokens.shape[0], qk_gain.shape[1]

    def swap(value, pairs):
        return lax.ppermute(value, "seq", pairs)

    w_in = jnp.transpose(w_qkv, (1, 0, 2))
    packed = pack(w_in, w_out)
    keep, send, inv = front(after(tokens, packed[0]), cotangent, modulation)
    come = swap(send, CORE_SWAP)
    came, ones, twos, fars, moved = list(packed), [], [], [], ()
    raws, wholes, kvs, qgs, pieces, chips = [], [], [], [], [], []

    def exchange(kv, *earlier):
        kv_chip = swap(after(kv, *earlier), CHIP_SWAP)
        chips.append(kv_chip)
        pieces.append([kv, swap(kv, CORE_SWAP), kv_chip])

    def slot(step, blocks, weights, earlier):
        own, away, whole = project(after(keep, *earlier), come, blocks, weights)
        raw, (kv,), (qg,) = finish(own, swap(away, CORE_SWAP), qk_gain)
        wholes.append(whole)
        raws.append(raw)
        kvs.append(around(kv, -step, count) if step else kv)
        qgs.append(around(qg, -step, count) if step else qg)

    slot(0, [], (w_in, w_out), ())
    for step in range(1, count):
        eight = [None] * 8
        for i in range(2):
            if step < count - 1:
                came[i] = around(after(came[i], *moved), 1, count)
            else:
                came[i] = around(after(packed[i], *moved), -1, count)
            moved = (came[i],)
            pace = [keep, *ones[-1:], *twos[-1:], *fars[:-1][-1:]]
            if i == 0 and step > 2:
                pace += [raws[step - 2]]
            own = after(came[i], *pace)
            ones.append(lax.ppermute(own, PLANE, plane_swap(True)))
            twos.append(lax.ppermute(own, PLANE, plane_swap(False)))
            fars.append(lax.ppermute(ones[-1], PLANE, plane_swap(False)))
            eight[4 * i : 4 * i + 4] = own, ones[-1], twos[-1], fars[-1]
        slot(step, [eight], (), (*kvs[1:], *qgs[1:]))
        if step == 1:
            exchange(jnp.concatenate(kvs, axis=0))
        elif step > 1:
            exchange(kvs[-1], *chips)
    pieces[-1][2] = after(pieces[-1][2], qgs[-1])
    pieces = [[*four, swap(four[2], CORE_SWAP)] for four in pieces]
    slots = range(count)
    dq, stay, send = attention(qgs, [p[i] for i in range(4) for p in pieces])
    dq = dq.reshape(count, rows, dim)
    dqs = [around(dq[i], i, count) if i else dq[i] for i in slots]
    summed = stay + swap(send, CORE_SWAP)
    came, *dqs = lax.optimization_barrier((swap(summed[1].astype(BF16), CHIP_SWAP), *dqs))
    dkv = (summed[0] + came.astype(F32)).astype(BF16).reshape(count, rows, 2 * dim)
    dkvs = [around(dkv[i], i, count) if i else dkv[i] for i in slots]

    dqkv = unfinish(qk_gain, raws, dqs, dkvs)
    own, away = back_project(dqkv, swap(dqkv, CORE_SWAP), wholes)
    return close(own, swap(away, CORE_SWAP), tokens, cotangent, modulation, inv)


def solution(mesh):
    placed = (
        P(("group", "seq", "tensor"), None),
        P(("group", "seq", "tensor"), None),
        P("group", None),
        P(None, None, "tensor"),
        P("tensor", None),
        P(),
    )
    sizes = dict(mesh.shape)

    def body(*args):
        weight_elements = args[3].size + args[4].size
        token_elements = 2 * 3 * args[0].size
        if sizes["group"] == 2 and sizes["seq"] == 4 and weight_elements < token_elements:
            return weight_gather_body(sizes["tensor"], *args)
        return token_gather_body(*args)

    return jax.shard_map(
        body,
        mesh=mesh,
        in_specs=placed,
        out_specs=P(("group", "seq", "tensor"), None),
        check_vma=False,
    )
```

```python
import math
from functools import partial

import jax
import jax.numpy as jnp
from jax import lax
from jax.experimental import pallas as pl
from jax.experimental.pallas import tpu as pltpu
from jax.sharding import PartitionSpec as P


def head_norm(raw, gain):
    scale_back = lax.rsqrt(jnp.mean(raw * raw, axis=-1, keepdims=True) + 1e-06)
    return (raw * scale_back * gain, scale_back)


def head_norm_back(raw, scale_back, gain, upstream):
    scaled_up = upstream * gain
    return scale_back * scaled_up - raw * scale_back**3 * jnp.mean(
        raw * scaled_up, axis=-1, keepdims=True
    )


def token_gather_body(tokens, cotangent, modulation, w_qkv, w_out, qk_gain):
    head_dim = qk_gain.shape[1]
    width = w_out.shape[0]
    nheads = width // head_dim
    model_width = tokens.shape[1]
    inv_sqrt = 1.0 / math.sqrt(head_dim)
    modulation_shift = modulation[0]
    modulation_scale = modulation[1]
    gate = modulation[2]
    input_rows_all = tokens.astype(jnp.float32)
    inverse_stddev = lax.rsqrt(
        jnp.mean(input_rows_all * input_rows_all, axis=-1, keepdims=True) + 1e-06
    )
    centered_normalized = input_rows_all * inverse_stddev
    layer_normed = (centered_normalized * (1.0 + modulation_scale) + modulation_shift).astype(
        jnp.bfloat16
    )
    cotangent_rows_all = cotangent.astype(jnp.float32)
    scaled_grad = (cotangent_rows_all * gate).astype(jnp.bfloat16)
    flat_in = w_qkv.reshape(model_width, 3 * width)
    qkv = jnp.dot(
        lax.all_gather(layer_normed, "tensor", axis=0, tiled=True),
        flat_in,
        preferred_element_type=jnp.float32,
    )
    rows = qkv.shape[0]
    query = qkv[:, :width].reshape(rows, nheads, head_dim)
    keys = qkv[:, width : 2 * width].reshape(rows, nheads, head_dim)
    values = qkv[:, 2 * width :].reshape(rows, nheads, head_dim)
    query_n, query_rs = head_norm(query, qk_gain[0])
    keys_n, keys_rs = head_norm(keys, qk_gain[1])
    query_b = query_n.astype(jnp.bfloat16)
    keys_b = keys_n.astype(jnp.bfloat16).reshape(rows, width)
    values_b = values.astype(jnp.bfloat16).reshape(rows, width)
    keys_all, values_all = (
        lax.all_gather(keys_b, "seq", axis=0, tiled=True),
        lax.all_gather(values_b, "seq", axis=0, tiled=True),
    )
    total = keys_all.shape[0]
    block = min(total, 512)
    count_blocks = total // block
    key_stack = keys_all.reshape(count_blocks, block, nheads, head_dim)
    value_stack = values_all.reshape(count_blocks, block, nheads, head_dim)

    def block_scores(queries, block_keys):
        return (
            jnp.einsum("qhd,khd->hqk", queries, block_keys, preferred_element_type=jnp.float32)
            * inv_sqrt
        )

    def stats_step(carry, block_keys):
        row_max, row_sum = carry
        scores = block_scores(query_b, block_keys)
        new_max = jnp.maximum(row_max, jnp.max(scores, axis=-1))
        row_sum = row_sum * jnp.exp(row_max - new_max) + jnp.sum(
            jnp.exp(scores - new_max[..., None]), axis=-1
        )
        return ((new_max, row_sum), None)

    start_max = jnp.full((nheads, rows), -jnp.inf, jnp.float32)
    start_sum = jnp.zeros((nheads, rows), jnp.float32)
    (row_max, row_sum), _ = lax.scan(stats_step, (start_max, start_sum), key_stack)

    def probs_of(scores, bmax, bsum):
        return jnp.exp(scores - bmax[..., None]) / bsum[..., None]

    def output_step(acc, pair):
        weights_b = probs_of(block_scores(query_b, pair[0]), row_max, row_sum).astype(jnp.bfloat16)
        return (
            acc
            + jnp.einsum("hqk,khd->hqd", weights_b, pair[1], preferred_element_type=jnp.float32),
            None,
        )

    attn_acc, _ = lax.scan(
        output_step, jnp.zeros((nheads, rows, head_dim), jnp.float32), (key_stack, value_stack)
    )
    attn_b = attn_acc.astype(jnp.bfloat16)
    dout = lax.dot_general(
        lax.all_gather(scaled_grad, "tensor", axis=0, tiled=True),
        w_out,
        (((1,), (1,)), ((), ())),
        preferred_element_type=jnp.float32,
    )
    grad_b = dout.astype(jnp.bfloat16)
    grad_q = grad_b.reshape(rows, nheads, head_dim)
    delta = jnp.sum(
        jnp.transpose(grad_q, (1, 0, 2)).astype(jnp.float32) * attn_b.astype(jnp.float32), axis=-1
    )

    def grad_terms(queries, grads, block_keys, block_values, bmax, bsum, bdelta):
        weights = probs_of(block_scores(queries, block_keys), bmax, bsum)
        dprob = jnp.einsum("qhd,khd->hqk", grads, block_values, preferred_element_type=jnp.float32)
        dscore = (weights * (dprob - bdelta[..., None])).astype(jnp.bfloat16)
        return (weights.astype(jnp.bfloat16), dscore)

    zeros_heads = jnp.zeros((nheads, rows, head_dim), jnp.float32)

    def both_step(acc, pair):
        weights_b, dscore = grad_terms(query_b, grad_q, pair[0], pair[1], row_max, row_sum, delta)
        acc = (
            acc
            + jnp.einsum("hqk,khd->hqd", dscore, pair[0], preferred_element_type=jnp.float32)
            * inv_sqrt
        )
        dkey_part = (
            jnp.einsum("hqk,qhd->khd", dscore, query_b, preferred_element_type=jnp.float32)
            * inv_sqrt
        )
        dvalue_part = jnp.einsum(
            "hqk,qhd->khd", weights_b, grad_q, preferred_element_type=jnp.float32
        )
        return (
            acc,
            jnp.concatenate(
                [dkey_part.reshape(block, width), dvalue_part.reshape(block, width)], axis=1
            ),
        )

    dquery, key_terms = lax.scan(both_step, zeros_heads, (key_stack, value_stack))
    own_terms = lax.psum_scatter(
        key_terms.reshape(total, 2 * width).astype(jnp.bfloat16),
        "seq",
        scatter_dimension=0,
        tiled=True,
    ).astype(jnp.float32)
    dkey = own_terms[:, :width].reshape(rows, nheads, head_dim)
    dvalue = own_terms[:, width:].reshape(rows, nheads, head_dim)
    dquery = jnp.transpose(dquery, (1, 0, 2))
    dq_raw = head_norm_back(query, query_rs, qk_gain[0], dquery)
    dk_raw = head_norm_back(keys, keys_rs, qk_gain[1], dkey)
    dqkv = jnp.concatenate(
        [dq_raw.reshape(rows, width), dk_raw.reshape(rows, width), dvalue.reshape(rows, width)],
        axis=1,
    ).astype(jnp.bfloat16)
    dnormed = lax.psum_scatter(
        lax.dot_general(
            dqkv, flat_in, (((1,), (1,)), ((), ())), preferred_element_type=jnp.float32
        ).astype(jnp.bfloat16),
        "tensor",
        scatter_dimension=0,
        tiled=True,
    ).astype(jnp.float32)
    normalized_grad = dnormed * (1.0 + modulation_scale)
    final_output = cotangent_rows_all + inverse_stddev * (
        normalized_grad
        - centered_normalized
        * jnp.mean(normalized_grad * centered_normalized, axis=-1, keepdims=True)
    )
    return final_output


CORE_SWAP = [(0, 1), (1, 0), (2, 3), (3, 2)]
CHIP_SWAP = [(0, 2), (2, 0), (1, 3), (3, 1)]
PLANE = ("group", "seq")


def plane_swap(first):
    pairs = []
    for group in range(2):
        for seq in range(4):
            along_chip = (seq % 2 == 0) == first
            to = group * 4 + (seq ^ 2) if along_chip else (1 - group) * 4 + seq
            pairs.append((group * 4 + seq, to))
    return pairs


def around(value, step, count):
    return lax.ppermute(value, "tensor", [(i, (i + step) % count) for i in range(count)])


def place():
    seq = lax.axis_index("seq")
    core, chip, group = seq & 1, seq >> 1, lax.axis_index("group")
    return core, chip, group, 2 * group + chip


def arrivals():
    core, chip, group, mine = place()
    across = 2 * group + (1 - chip)
    over = 2 * (1 - group) + chip
    return mine, jnp.where(core == 0, across, over), jnp.where(core == 0, over, across), 3 - mine


def call(kernel, name, out, operands, megabytes, far=(), scratch=()):
    vmem = pl.BlockSpec(memory_space=pltpu.VMEM)
    hbm = pl.BlockSpec(memory_space=pltpu.HBM)
    out = tuple(jax.ShapeDtypeStruct(shape, dtype) for shape, dtype in out)
    return pl.pallas_call(
        kernel,
        out_shape=out,
        in_specs=[hbm if i in far else vmem for i in range(len(operands))],
        out_specs=(vmem,) * len(out),
        scratch_shapes=list(scratch),
        compiler_params=pltpu.CompilerParams(vmem_limit_bytes=megabytes and megabytes * 1024 * 1024),
        cost_estimate=pl.CostEstimate(flops=0, bytes_accessed=0, transcendentals=0),
        name=name,
    )(*operands)


BF16, F32 = jnp.bfloat16, jnp.float32
NT = (((1,), (1,)), ((), ()))
TN = (((0,), (0,)), ((), ()))


def pack_kernel(w_in, w_out, packed, quarter, sems):
    core, _, _, mine = place()
    part, dim = packed.shape[1:]
    half, tile = 4 * part, dim // 4
    rows = pl.ds(pl.multiple_of(core * half + mine * part, tile), part)
    copies = [pltpu.make_async_copy(w_in.at[j, rows, :], packed.at[j], sems.at[j]) for j in range(3)]
    lanes = pl.ds(pl.multiple_of(core * half, dim), half)
    heads = pl.ds(pl.multiple_of(mine * tile, tile), tile)
    copies.append(pltpu.make_async_copy(w_out.at[heads, lanes], quarter, sems.at[3]))
    for copy in copies:
        copy.start()
    for copy in reversed(copies):
        copy.wait()
    for i in range(part // tile):
        packed[3, i * tile : (i + 1) * tile, :] = quarter[:, i * dim : (i + 1) * dim]


def pack(w_in, w_out):
    _, width, dim = w_in.shape
    part = width // 8
    return call(
        pack_kernel,
        "pack",
        [((4, part, dim), BF16)],
        (w_in, w_out),
        60,
        far=(0, 1),
        scratch=[pltpu.VMEM((dim // 4, 4 * part), BF16), pltpu.SemaphoreType.DMA((4,))],
    )[0]


def front_kernel(x_ref, c_ref, mod_ref, keep_ref, send_ref, inv_ref):
    half = keep_ref.shape[1] // 2
    core = place()[0]
    x = x_ref[...].astype(F32)
    inv = lax.rsqrt(jnp.mean(x * x, axis=-1, keepdims=True) + 1e-06)
    inv_ref[...] = inv
    for i in range(2):
        at = pl.ds(i * half, half)
        xhat = x_ref[:, at].astype(F32) * inv
        normed = (xhat * (1.0 + mod_ref[1:2, at]) + mod_ref[0:1, at]).astype(BF16)
        scaled = (c_ref[:, at].astype(F32) * mod_ref[2:3, at]).astype(BF16)

        @pl.when(core == i)
        def _():
            keep_ref[:, :half] = normed
            keep_ref[:, half:] = scaled

        @pl.when(core != i)
        def _():
            send_ref[:, :half] = normed
            send_ref[:, half:] = scaled


def front(tokens, cotangent, modulation):
    return call(
        front_kernel,
        "front",
        [(tokens.shape, BF16), (tokens.shape, BF16), ((tokens.shape[0], 1), F32)],
        (tokens, cotangent, modulation),
        12,
    )


def project_kernel(first, keep_ref, come_ref, *refs):
    rows, half = keep_ref.shape[0], keep_ref.shape[1] // 2
    if first:
        w_in, w_out, own_ref, away_ref, whole, whole_out, sems = refs
        dim = w_in.shape[2]
        at = pl.ds(pl.multiple_of(place()[0] * half, dim), half)
        copies = [
            pltpu.make_async_copy(w_in.at[j, at, :], whole.at[:, j * dim : (j + 1) * dim], sems.at[j])
            for j in range(3)
        ]
        copies.append(pltpu.make_async_copy(w_out.at[:, at], whole_out, sems.at[3]))
        for copy in copies:
            copy.start()
        for copy in copies:
            copy.wait()
    else:
        *blocks, own_ref, away_ref, whole, whole_out = refs
        dim = whole_out.shape[0]
        tile = dim // 4
        for block, at in zip(blocks, arrivals()):
            part = block.shape[1]
            to = pl.ds(pl.multiple_of(at * part, tile), part)
            for j in range(3):
                whole[to, j * dim : (j + 1) * dim] = block[j]
            to = pl.ds(pl.multiple_of(at * tile, tile), tile)
            for t in range(part // tile):
                whole_out[to, t * dim : (t + 1) * dim] = block[3, t * tile : (t + 1) * tile, :]
    x = jnp.concatenate([keep_ref[...], come_ref[...]], axis=0)
    qkv = jnp.dot(x[:, :half], whole[...], preferred_element_type=F32)
    grad = lax.dot_general(x[:, half:], whole_out[...], NT, preferred_element_type=F32)
    own_ref[:, : 3 * dim] = qkv[:rows]
    own_ref[:, 3 * dim :] = grad[:rows]
    away_ref[:, : 3 * dim] = qkv[rows:]
    away_ref[:, 3 * dim :] = grad[rows:]


def project(keep, come, blocks, weights=()):
    rows, half = keep.shape[0], keep.shape[1] // 2
    first = len(weights) == 2
    dim = (*weights, *blocks)[0].shape[2]
    sums = ((rows, 4 * dim), F32)
    return call(
        partial(project_kernel, first),
        "project",
        [sums, sums, ((half, 3 * dim), BF16)],
        (keep, come, *weights, *blocks),
        12,
        far=(2, 3) if first else (),
        scratch=[pltpu.VMEM((dim, half), BF16)] + [pltpu.SemaphoreType.DMA((4,))] * first,
    )


def unit(raw):
    back = lax.rsqrt(jnp.mean(raw * raw, axis=-1, keepdims=True) + 1e-06)
    return raw * back, back


def finish_kernel(own_ref, come_ref, gain_ref, raw_ref, *refs):
    dim = gain_ref.shape[1]
    raw = own_ref[...] + come_ref[...]
    raw_ref[...] = raw[:, : 2 * dim]
    qh, _ = unit(raw[:, :dim])
    kh, _ = unit(raw[:, dim : 2 * dim])
    kv_ref, qg_ref, at = refs[0], refs[-1], 2 * dim * (2 - len(refs))
    kv_ref[:, :dim] = (kh * gain_ref[1:2, :]).astype(BF16)
    kv_ref[:, dim : 2 * dim] = raw[:, 2 * dim : 3 * dim].astype(BF16)
    qg_ref[:, at : at + dim] = (qh * gain_ref[0:1, :]).astype(BF16)
    qg_ref[:, at + dim :] = raw[:, 3 * dim :].astype(BF16)


def finish(own, come, gains, joined):
    rows, dim = own.shape[0], gains.shape[1]
    ready = [((rows, 4 * dim), BF16)] if joined else [((rows, 2 * dim), BF16)] * 2
    return call(finish_kernel, "finish", [((rows, 2 * dim), F32)] + ready, (own, come, gains), 6)


def attention_kernel(scale, block, slots, *refs):
    qgs, kvs = refs[:slots], refs[slots:-9]
    dq_ref, stay_ref, send_ref, q_ref, g_ref, k_ref, v_ref, prob_ref, dprob_ref = refs[-9:]
    total, dim = k_ref.shape
    rows = q_ref.shape[0]
    steps = total // block
    for i, qg in enumerate(qgs):
        at = pl.ds(i * qg.shape[0], qg.shape[0])
        q_ref[at, :] = qg[:, -2 * dim : -dim]
        g_ref[at, :] = qg[:, -dim:]
    at = 0
    for kv in kvs:
        k_ref[pl.ds(at, kv.shape[0]), :] = kv[:, :dim]
        v_ref[pl.ds(at, kv.shape[0]), :] = kv[:, dim:]
        at += kv.shape[0]

    def scores(i, top):
        here = pl.ds(pl.multiple_of(i * block, block), block)
        s = lax.dot_general(k_ref[here, :], q_ref[...], NT, preferred_element_type=F32) * scale
        prob_ref[here, :] = s
        dprob_ref[here, :] = lax.dot_general(
            v_ref[here, :], g_ref[...], NT, preferred_element_type=F32
        )
        return jnp.maximum(top, jnp.max(s, axis=0, keepdims=True))

    top = lax.fori_loop(0, steps, scores, jnp.full((1, rows), -jnp.inf, F32))

    def weigh(i, carry):
        norm, cross = carry
        here = pl.ds(pl.multiple_of(i * block, block), block)
        e = jnp.exp(prob_ref[here, :] - top)
        prob_ref[here, :] = e
        return (
            norm + jnp.sum(e, axis=0, keepdims=True),
            cross + jnp.sum(e * dprob_ref[here, :], axis=0, keepdims=True),
        )

    none = jnp.zeros((1, rows), F32)
    norm, cross = lax.fori_loop(0, steps, weigh, (none, none))
    inverse = 1.0 / norm
    delta = cross * inverse
    dq = jnp.zeros((dim, rows), F32)
    quarter = total // 4
    for turn in range(4):
        out_ref = (stay_ref, send_ref)[turn % 2]

        def back(i, dq):
            here = pl.ds(pl.multiple_of(turn * quarter + i * block, block), block)
            to = pl.ds(pl.multiple_of(i * block, block), block)
            p = prob_ref[here, :] * inverse
            ds = (p * (dprob_ref[here, :] - delta)).astype(BF16)
            dk = jnp.dot(ds, q_ref[...], preferred_element_type=F32) * scale
            dv = jnp.dot(p.astype(BF16), g_ref[...], preferred_element_type=F32)
            out_ref[turn // 2, to, :dim] = dk.astype(out_ref.dtype)
            out_ref[turn // 2, to, dim:] = dv.astype(out_ref.dtype)
            return dq + lax.dot_general(k_ref[here, :], ds, TN, preferred_element_type=F32)

        dq = lax.fori_loop(0, quarter // block, back, dq)
    dq_ref[...] = (dq.T * scale).astype(BF16)


def attention(qgs, pieces):
    slots, dim = len(qgs), pieces[0][0].shape[1] // 2
    rows = sum(qg.shape[0] for qg in qgs)
    total = 4 * rows
    terms = (2, rows, 2 * dim)
    return call(
        partial(attention_kernel, 1.0 / math.sqrt(dim), rows // 2, slots),
        "attention",
        [((rows, dim), BF16), (terms, F32), (terms, BF16)],
        [*qgs, *[piece for some in pieces for piece in some]],
        24,
        scratch=[pltpu.VMEM((rows, dim), BF16)] * 2
        + [pltpu.VMEM((total, dim), BF16)] * 2
        + [pltpu.VMEM((total, rows), F32)] * 2,
    )


def unfinish_kernel(slots, gain_ref, *refs):
    raws, dqs, dkvs = refs[:slots], refs[slots : 2 * slots], refs[2 * slots : 3 * slots]
    out_ref = refs[-1]
    dim = gain_ref.shape[1]

    def unit_back(raw, gain, upstream):
        hat, scale_back = unit(raw)
        up = upstream.astype(F32) * gain
        return scale_back * (up - hat * jnp.mean(up * hat, axis=-1, keepdims=True))

    for i, (raw, dq, dkv) in enumerate(zip(raws, dqs, dkvs)):
        at = 3 * dim * i
        dq = unit_back(raw[:, :dim], gain_ref[0:1, :], dq[...])
        dk = unit_back(raw[:, dim:], gain_ref[1:2, :], dkv[:, :dim])
        out_ref[:, at : at + dim] = dq.astype(BF16)
        out_ref[:, at + dim : at + 2 * dim] = dk.astype(BF16)
        out_ref[:, at + 2 * dim : at + 3 * dim] = dkv[:, dim:]


def unfinish(gains, raws, dqs, dkvs):
    slots, (rows, dim) = len(dqs), dqs[0].shape
    return call(
        partial(unfinish_kernel, slots),
        "unfinish",
        [((rows, 3 * dim * slots), BF16)],
        (gains, *raws, *dqs, *dkvs),
        6,
    )[0]


def back_project_kernel(grads, *refs):
    weights, out_ref = refs[:-1], refs[-1]
    half = out_ref.shape[1]
    width = grads.shape[1] // len(weights)
    step = half // 7 if half % 7 == 0 else half
    for to in range(0, half, step):
        total = None
        for i, whole in enumerate(weights):
            part = lax.dot_general(
                grads[:, width * i : width * (i + 1)],
                whole[to : to + step, :],
                NT,
                preferred_element_type=F32,
            )
            total = part if total is None else total + part
        out_ref[:, to : to + step] = total.astype(out_ref.dtype)


def back_project(grads, weights, dtype):
    shape = grads.shape[0], weights[0].shape[0]
    return call(back_project_kernel, "back_project", [(shape, dtype)], (grads, *weights), 16)[0]


def close_kernel(own_ref, away_ref, x_ref, c_ref, mod_ref, inv_ref, out_ref):
    half = own_ref.shape[1]
    core = place()[0]
    inv = inv_ref[...]
    total = 0.0
    for i in range(2):
        at = pl.ds(i * half, half)
        grad = jnp.where(core == i, own_ref[...], away_ref[...].astype(F32))
        dhat = grad * (1.0 + mod_ref[1:2, at])
        out_ref[:, at] = dhat
        total += jnp.sum(dhat * x_ref[:, at].astype(F32), axis=-1, keepdims=True)
    cross = total * (inv * inv * (0.5 / half))
    for i in range(2):
        at = pl.ds(i * half, half)
        dhat = out_ref[:, at] - x_ref[:, at].astype(F32) * cross
        out_ref[:, at] = c_ref[:, at].astype(F32) + inv * dhat


def close(own, away, tokens, cotangent, modulation, inv):
    return call(
        close_kernel,
        "close",
        [(tokens.shape, F32)],
        (own, away, tokens, cotangent, modulation, inv),
        12,
    )[0]


def after(value, *earlier):
    return lax.optimization_barrier((value, *earlier))[0]


def weight_gather_body(count, tokens, cotangent, modulation, w_qkv, w_out, qk_gain):
    rows, dim = tokens.shape[0], qk_gain.shape[1]

    def swap(value, pairs):
        return lax.ppermute(value, "seq", pairs)

    w_in = jnp.transpose(w_qkv, (1, 0, 2))
    packed = pack(w_in, w_out)
    keep, send, inv = front(after(tokens, packed), cotangent, modulation)
    came, swaps = packed, []
    raws, wholes, heads = [], [], []

    def in_plane(value, axes, pairs, *earlier):
        swaps.append(lax.ppermute(after(value, *swaps[:-2][-1:], *earlier), axes, pairs))
        return swaps[-1]

    def slot(step, blocks, weights, *earlier):
        own, away, whole = project(after(keep, *earlier), come, blocks, weights)
        raw, *head = finish(own, swap(away, CORE_SWAP), qk_gain, step < count - 1)
        wholes.append(whole)
        raws.append(raw)
        heads.append(head)

    def across(value, step):
        pairs = [(4 * t + s, (t + step) % count * 4 + (s ^ 2)) for t in range(count) for s in range(4)]
        return lax.ppermute(value, ("tensor", "seq"), pairs)

    def home(step, *earlier):
        for i, part in enumerate(heads[step]):
            heads[step][i] = around(after(part, *earlier), -step, count)
            earlier = (heads[step][i],)
        return earlier

    for step in range(1, count):
        last = step == count - 1
        came = around(after(packed, came), -1, count) if last else around(came, 1, count)
        if step == 1:
            come = swap(after(send, came), CORE_SWAP)
        one = in_plane(came, PLANE, plane_swap(True), *([keep] if step == 1 else raws[: step - 1]))
        sent = home(1, came) if last else ()
        two = in_plane(came, PLANE, plane_swap(False), *sent)
        far = in_plane(one, PLANE, plane_swap(False), *([two, raws[-1]] if last else ()))
        if step == 1:
            slot(0, [], (w_in, w_out))
        if last:
            for i in range(2, step):
                sent = home(i, *sent)
        slot(step, [came, one, two, far], (), *sent)
    kv, qg = after(heads[-1][0], *sent), after(heads[-1][1], *sent)
    turned = across(kv, 1 - count)
    heads[-1] = [around(kv, 1 - count, count), around(qg, 1 - count, count)]

    kv = jnp.concatenate([head[0][:, : 2 * dim] for head in heads[:-1]], axis=0)
    pieces = [[kv, swap(kv, CORE_SWAP), in_plane(kv, "seq", CHIP_SWAP)]]
    kv = heads[-1][0]
    pieces.append([kv, swap(kv, CORE_SWAP), turned])
    pieces[0][2] = after(pieces[0][2], *heads[-1], turned)
    pieces = [[*four, swap(four[2], CORE_SWAP)] for four in pieces]
    pieces = [[four[i] for four in pieces] for i in range(4)]
    qgs = [head[-1] for head in heads]
    slots = range(count)
    dq, stay, send = attention(qgs, pieces)
    dq = dq.reshape(count, rows, dim)
    dqs = [around(dq[i], i, count) if i else dq[i] for i in slots]
    summed = stay + swap(send, CORE_SWAP).astype(F32)
    came, *dqs = lax.optimization_barrier((swap(summed[1].astype(BF16), CHIP_SWAP), *dqs))
    dkv = (summed[0] + came.astype(F32)).astype(BF16).reshape(count, rows, 2 * dim)
    dkvs = [around(dkv[i], i, count) if i else dkv[i] for i in slots]

    dqkv = unfinish(qk_gain, raws, dqs, dkvs)
    away = swap(back_project(swap(dqkv, CORE_SWAP), wholes, BF16), CORE_SWAP)
    return close(back_project(dqkv, wholes, F32), away, tokens, cotangent, modulation, inv)


def solution(mesh):
    placed = (
        P(("group", "seq", "tensor"), None),
        P(("group", "seq", "tensor"), None),
        P("group", None),
        P(None, None, "tensor"),
        P("tensor", None),
        P(),
    )
    sizes = dict(mesh.shape)

    def body(*args):
        weight_elements = args[3].size + args[4].size
        token_elements = 2 * 3 * args[0].size
        if sizes["group"] == 2 and sizes["seq"] == 4 and weight_elements < token_elements:
            return weight_gather_body(sizes["tensor"], *args)
        return token_gather_body(*args)

    return jax.shard_map(
        body,
        mesh=mesh,
        in_specs=placed,
        out_specs=P(("group", "seq", "tensor"), None),
        check_vma=False,
    )
```

```python
import math
from functools import partial

import jax
import jax.numpy as jnp
from jax import lax
from jax.experimental import pallas as pl
from jax.experimental.pallas import tpu as pltpu
from jax.sharding import PartitionSpec as P


def head_norm(raw, gain):
    scale_back = lax.rsqrt(jnp.mean(raw * raw, axis=-1, keepdims=True) + 1e-06)
    return (raw * scale_back * gain, scale_back)


def head_norm_back(raw, scale_back, gain, upstream):
    scaled_up = upstream * gain
    return scale_back * scaled_up - raw * scale_back**3 * jnp.mean(
        raw * scaled_up, axis=-1, keepdims=True
    )


def token_gather_body(tokens, cotangent, modulation, w_qkv, w_out, qk_gain):
    head_dim = qk_gain.shape[1]
    width = w_out.shape[0]
    nheads = width // head_dim
    model_width = tokens.shape[1]
    inv_sqrt = 1.0 / math.sqrt(head_dim)
    modulation_shift = modulation[0]
    modulation_scale = modulation[1]
    gate = modulation[2]
    input_rows_all = tokens.astype(jnp.float32)
    inverse_stddev = lax.rsqrt(
        jnp.mean(input_rows_all * input_rows_all, axis=-1, keepdims=True) + 1e-06
    )
    centered_normalized = input_rows_all * inverse_stddev
    layer_normed = (centered_normalized * (1.0 + modulation_scale) + modulation_shift).astype(
        jnp.bfloat16
    )
    cotangent_rows_all = cotangent.astype(jnp.float32)
    scaled_grad = (cotangent_rows_all * gate).astype(jnp.bfloat16)
    flat_in = w_qkv.reshape(model_width, 3 * width)
    qkv = jnp.dot(
        lax.all_gather(layer_normed, "tensor", axis=0, tiled=True),
        flat_in,
        preferred_element_type=jnp.float32,
    )
    rows = qkv.shape[0]
    query = qkv[:, :width].reshape(rows, nheads, head_dim)
    keys = qkv[:, width : 2 * width].reshape(rows, nheads, head_dim)
    values = qkv[:, 2 * width :].reshape(rows, nheads, head_dim)
    query_n, query_rs = head_norm(query, qk_gain[0])
    keys_n, keys_rs = head_norm(keys, qk_gain[1])
    query_b = query_n.astype(jnp.bfloat16)
    keys_b = keys_n.astype(jnp.bfloat16).reshape(rows, width)
    values_b = values.astype(jnp.bfloat16).reshape(rows, width)
    keys_all, values_all = (
        lax.all_gather(keys_b, "seq", axis=0, tiled=True),
        lax.all_gather(values_b, "seq", axis=0, tiled=True),
    )
    total = keys_all.shape[0]
    block = min(total, 512)
    count_blocks = total // block
    key_stack = keys_all.reshape(count_blocks, block, nheads, head_dim)
    value_stack = values_all.reshape(count_blocks, block, nheads, head_dim)

    def block_scores(queries, block_keys):
        return (
            jnp.einsum("qhd,khd->hqk", queries, block_keys, preferred_element_type=jnp.float32)
            * inv_sqrt
        )

    def stats_step(carry, block_keys):
        row_max, row_sum = carry
        scores = block_scores(query_b, block_keys)
        new_max = jnp.maximum(row_max, jnp.max(scores, axis=-1))
        row_sum = row_sum * jnp.exp(row_max - new_max) + jnp.sum(
            jnp.exp(scores - new_max[..., None]), axis=-1
        )
        return ((new_max, row_sum), None)

    start_max = jnp.full((nheads, rows), -jnp.inf, jnp.float32)
    start_sum = jnp.zeros((nheads, rows), jnp.float32)
    (row_max, row_sum), _ = lax.scan(stats_step, (start_max, start_sum), key_stack)

    def probs_of(scores, bmax, bsum):
        return jnp.exp(scores - bmax[..., None]) / bsum[..., None]

    def output_step(acc, pair):
        weights_b = probs_of(block_scores(query_b, pair[0]), row_max, row_sum).astype(jnp.bfloat16)
        return (
            acc
            + jnp.einsum("hqk,khd->hqd", weights_b, pair[1], preferred_element_type=jnp.float32),
            None,
        )

    attn_acc, _ = lax.scan(
        output_step, jnp.zeros((nheads, rows, head_dim), jnp.float32), (key_stack, value_stack)
    )
    attn_b = attn_acc.astype(jnp.bfloat16)
    dout = lax.dot_general(
        lax.all_gather(scaled_grad, "tensor", axis=0, tiled=True),
        w_out,
        (((1,), (1,)), ((), ())),
        preferred_element_type=jnp.float32,
    )
    grad_b = dout.astype(jnp.bfloat16)
    grad_q = grad_b.reshape(rows, nheads, head_dim)
    delta = jnp.sum(
        jnp.transpose(grad_q, (1, 0, 2)).astype(jnp.float32) * attn_b.astype(jnp.float32), axis=-1
    )

    def grad_terms(queries, grads, block_keys, block_values, bmax, bsum, bdelta):
        weights = probs_of(block_scores(queries, block_keys), bmax, bsum)
        dprob = jnp.einsum("qhd,khd->hqk", grads, block_values, preferred_element_type=jnp.float32)
        dscore = (weights * (dprob - bdelta[..., None])).astype(jnp.bfloat16)
        return (weights.astype(jnp.bfloat16), dscore)

    zeros_heads = jnp.zeros((nheads, rows, head_dim), jnp.float32)

    def both_step(acc, pair):
        weights_b, dscore = grad_terms(query_b, grad_q, pair[0], pair[1], row_max, row_sum, delta)
        acc = (
            acc
            + jnp.einsum("hqk,khd->hqd", dscore, pair[0], preferred_element_type=jnp.float32)
            * inv_sqrt
        )
        dkey_part = (
            jnp.einsum("hqk,qhd->khd", dscore, query_b, preferred_element_type=jnp.float32)
            * inv_sqrt
        )
        dvalue_part = jnp.einsum(
            "hqk,qhd->khd", weights_b, grad_q, preferred_element_type=jnp.float32
        )
        return (
            acc,
            jnp.concatenate(
                [dkey_part.reshape(block, width), dvalue_part.reshape(block, width)], axis=1
            ),
        )

    dquery, key_terms = lax.scan(both_step, zeros_heads, (key_stack, value_stack))
    own_terms = lax.psum_scatter(
        key_terms.reshape(total, 2 * width).astype(jnp.bfloat16),
        "seq",
        scatter_dimension=0,
        tiled=True,
    ).astype(jnp.float32)
    dkey = own_terms[:, :width].reshape(rows, nheads, head_dim)
    dvalue = own_terms[:, width:].reshape(rows, nheads, head_dim)
    dquery = jnp.transpose(dquery, (1, 0, 2))
    dq_raw = head_norm_back(query, query_rs, qk_gain[0], dquery)
    dk_raw = head_norm_back(keys, keys_rs, qk_gain[1], dkey)
    dqkv = jnp.concatenate(
        [dq_raw.reshape(rows, width), dk_raw.reshape(rows, width), dvalue.reshape(rows, width)],
        axis=1,
    ).astype(jnp.bfloat16)
    dnormed = lax.psum_scatter(
        lax.dot_general(
            dqkv, flat_in, (((1,), (1,)), ((), ())), preferred_element_type=jnp.float32
        ).astype(jnp.bfloat16),
        "tensor",
        scatter_dimension=0,
        tiled=True,
    ).astype(jnp.float32)
    normalized_grad = dnormed * (1.0 + modulation_scale)
    final_output = cotangent_rows_all + inverse_stddev * (
        normalized_grad
        - centered_normalized
        * jnp.mean(normalized_grad * centered_normalized, axis=-1, keepdims=True)
    )
    return final_output


CORE_SWAP = [(0, 1), (1, 0), (2, 3), (3, 2)]
CHIP_SWAP = [(0, 2), (2, 0), (1, 3), (3, 1)]
PLANE = ("group", "seq")


def plane_swap(first):
    pairs = []
    for group in range(2):
        for seq in range(4):
            along_chip = (seq % 2 == 0) == first
            to = group * 4 + (seq ^ 2) if along_chip else (1 - group) * 4 + seq
            pairs.append((group * 4 + seq, to))
    return pairs


def around(value, step, count):
    return lax.ppermute(value, "tensor", [(i, (i + step) % count) for i in range(count)])


def place():
    seq = lax.axis_index("seq")
    core, chip, group = seq & 1, seq >> 1, lax.axis_index("group")
    return core, chip, group, 2 * group + chip


def arrivals():
    core, chip, group, mine = place()
    across = 2 * group + (1 - chip)
    over = 2 * (1 - group) + chip
    return mine, jnp.where(core == 0, across, over), jnp.where(core == 0, over, across), 3 - mine


def call(kernel, name, out, operands, megabytes, far=(), scratch=()):
    vmem = pl.BlockSpec(memory_space=pltpu.VMEM)
    hbm = pl.BlockSpec(memory_space=pltpu.HBM)
    out = tuple(jax.ShapeDtypeStruct(shape, dtype) for shape, dtype in out)
    return pl.pallas_call(
        kernel,
        out_shape=out,
        in_specs=[hbm if i in far else vmem for i in range(len(operands))],
        out_specs=(vmem,) * len(out),
        scratch_shapes=list(scratch),
        compiler_params=pltpu.CompilerParams(vmem_limit_bytes=megabytes and megabytes * 1024 * 1024),
        cost_estimate=pl.CostEstimate(flops=0, bytes_accessed=0, transcendentals=0),
        name=name,
    )(*operands)


BF16, F32 = jnp.bfloat16, jnp.float32
NT = (((1,), (1,)), ((), ()))
TN = (((0,), (0,)), ((), ()))


def pack_kernel(w_in, w_out, near, second, quarters, sems):
    core = place()[0]
    part, dim = near.shape[1:]
    half, tile = 4 * part, dim // 4
    lanes = pl.ds(pl.multiple_of(core * half, dim), half)
    copies = []
    for i, (packed, at) in enumerate(((near, arrivals()[0]), (second, arrivals()[2]))):
        rows = pl.ds(pl.multiple_of(core * half + at * part, tile), part)
        heads = pl.ds(pl.multiple_of(at * tile, tile), tile)
        pairs = [(w_in.at[j, rows, :], packed.at[j]) for j in range(3)]
        pairs.append((w_out.at[heads, lanes], quarters.at[i]))
        copies += [pltpu.make_async_copy(s, d, sems.at[4 * i + j]) for j, (s, d) in enumerate(pairs)]
    for copy in copies:
        copy.start()
    for copy in copies:
        copy.wait()
    for i, packed in enumerate((near, second)):
        for t in range(part // tile):
            packed[3, t * tile : (t + 1) * tile, :] = quarters[i, :, t * dim : (t + 1) * dim]


def pack(w_in, w_out):
    _, width, dim = w_in.shape
    part = width // 8
    return call(
        pack_kernel,
        "pack",
        [((4, part, dim), BF16)] * 2,
        (w_in, w_out),
        60,
        far=(0, 1),
        scratch=[pltpu.VMEM((2, dim // 4, 4 * part), BF16), pltpu.SemaphoreType.DMA((8,))],
    )


def front_kernel(x_ref, c_ref, mod_ref, keep_ref, send_ref, inv_ref):
    half = keep_ref.shape[1] // 2
    core = place()[0]
    x = x_ref[...].astype(F32)
    inv = lax.rsqrt(jnp.mean(x * x, axis=-1, keepdims=True) + 1e-06)
    inv_ref[...] = inv
    for i in range(2):
        at = pl.ds(i * half, half)
        xhat = x_ref[:, at].astype(F32) * inv
        normed = (xhat * (1.0 + mod_ref[1:2, at]) + mod_ref[0:1, at]).astype(BF16)
        scaled = (c_ref[:, at].astype(F32) * mod_ref[2:3, at]).astype(BF16)

        @pl.when(core == i)
        def _():
            keep_ref[:, :half] = normed
            keep_ref[:, half:] = scaled

        @pl.when(core != i)
        def _():
            send_ref[:, :half] = normed
            send_ref[:, half:] = scaled


def front(tokens, cotangent, modulation):
    return call(
        front_kernel,
        "front",
        [(tokens.shape, BF16), (tokens.shape, BF16), ((tokens.shape[0], 1), F32)],
        (tokens, cotangent, modulation),
        12,
    )


def project_kernel(first, keep_ref, come_ref, *refs):
    rows, half = keep_ref.shape[0], keep_ref.shape[1] // 2
    if first:
        w_in, w_out, own_ref, away_ref, whole, whole_out, sems = refs
        dim = w_in.shape[2]
        at = pl.ds(pl.multiple_of(place()[0] * half, dim), half)
        copies = [
            pltpu.make_async_copy(w_in.at[j, at, :], whole.at[:, j * dim : (j + 1) * dim], sems.at[j])
            for j in range(3)
        ]
        copies.append(pltpu.make_async_copy(w_out.at[:, at], whole_out, sems.at[3]))
        for copy in copies:
            copy.start()
        for copy in copies:
            copy.wait()
    else:
        *blocks, own_ref, away_ref, whole, whole_out = refs
        dim = whole_out.shape[0]
        tile = dim // 4
        for block, at in zip(blocks, arrivals()):
            part = block.shape[1]
            to = pl.ds(pl.multiple_of(at * part, tile), part)
            for j in range(3):
                whole[to, j * dim : (j + 1) * dim] = block[j]
            to = pl.ds(pl.multiple_of(at * tile, tile), tile)
            for t in range(part // tile):
                whole_out[to, t * dim : (t + 1) * dim] = block[3, t * tile : (t + 1) * tile, :]
    x = jnp.concatenate([keep_ref[...], come_ref[...]], axis=0)
    qkv = jnp.dot(x[:, :half], whole[...], preferred_element_type=F32)
    grad = lax.dot_general(x[:, half:], whole_out[...], NT, preferred_element_type=F32)
    own_ref[:, : 3 * dim] = qkv[:rows]
    own_ref[:, 3 * dim :] = grad[:rows]
    away_ref[:, : 3 * dim] = qkv[rows:]
    away_ref[:, 3 * dim :] = grad[rows:]


def project(keep, come, blocks, weights=()):
    rows, half = keep.shape[0], keep.shape[1] // 2
    first = len(weights) == 2
    dim = (*weights, *blocks)[0].shape[2]
    sums = ((rows, 4 * dim), F32)
    return call(
        partial(project_kernel, first),
        "project",
        [sums, sums, ((half, 3 * dim), BF16)],
        (keep, come, *weights, *blocks),
        12,
        far=(2, 3) if first else (),
        scratch=[pltpu.VMEM((dim, half), BF16)] + [pltpu.SemaphoreType.DMA((4,))] * first,
    )


def unit(raw):
    back = lax.rsqrt(jnp.mean(raw * raw, axis=-1, keepdims=True) + 1e-06)
    return raw * back, back


def finish_kernel(own_ref, come_ref, gain_ref, raw_ref, *refs):
    dim = gain_ref.shape[1]
    raw = own_ref[...] + come_ref[...]
    raw_ref[...] = raw[:, : 2 * dim]
    qh, _ = unit(raw[:, :dim])
    kh, _ = unit(raw[:, dim : 2 * dim])
    kv_ref, qg_ref, at = refs[0], refs[-1], 2 * dim * (2 - len(refs))
    kv_ref[:, :dim] = (kh * gain_ref[1:2, :]).astype(BF16)
    kv_ref[:, dim : 2 * dim] = raw[:, 2 * dim : 3 * dim].astype(BF16)
    qg_ref[:, at : at + dim] = (qh * gain_ref[0:1, :]).astype(BF16)
    qg_ref[:, at + dim :] = raw[:, 3 * dim :].astype(BF16)


def finish(own, come, gains, joined):
    rows, dim = own.shape[0], gains.shape[1]
    ready = [((rows, 4 * dim), BF16)] if joined else [((rows, 2 * dim), BF16)] * 2
    return call(finish_kernel, "finish", [((rows, 2 * dim), F32)] + ready, (own, come, gains), 6)


def key_terms(scale, at, rows, q_ref, g_ref, k_ref, prob_ref, dprob_ref, inverse, delta):
    here = pl.ds(at, rows)
    p = prob_ref[here, :] * inverse
    ds = (p * (dprob_ref[here, :] - delta)).astype(BF16)
    dk = jnp.dot(ds, q_ref[...], preferred_element_type=F32) * scale
    dv = jnp.dot(p.astype(BF16), g_ref[...], preferred_element_type=F32)
    dq = lax.dot_general(k_ref[here, :], ds, TN, preferred_element_type=F32)
    return jnp.concatenate([dk, dv], axis=1), dq


def attention_kernel(scale, slots, *refs):
    qgs, kvs = refs[:slots], refs[slots:-15]
    stay_ref, send_ref, q_ref, g_ref, near_k_ref, near_prob_ref, near_dprob_ref = refs[-15:-8]
    stats_ref, dq_ref, near_v_ref, far_k_ref, far_v_ref, far_prob_ref, far_dprob_ref = refs[-8:-1]
    top_ref = refs[-1]
    rows, dim = q_ref.shape
    for i, qg in enumerate(qgs):
        at = pl.ds(i * qg.shape[0], qg.shape[0])
        q_ref[at, :] = qg[:, -2 * dim : -dim]
        g_ref[at, :] = qg[:, -dim:]
    at = 0
    for kv in kvs:
        size = kv.shape[0]
        k_ref, v_ref = ((near_k_ref, near_v_ref), (far_k_ref, far_v_ref))[at // (2 * rows)]
        to = pl.ds(at % (2 * rows), size)
        k_ref[to, :] = kv[:, :dim]
        v_ref[to, :] = kv[:, dim:]
        at += size
    near = (near_k_ref, near_v_ref, near_prob_ref, near_dprob_ref)
    far = (far_k_ref, far_v_ref, far_prob_ref, far_dprob_ref)
    top = jnp.full((1, rows), -jnp.inf, F32)
    for k_ref, v_ref, prob_ref, dprob_ref in (near, far):

        def scores(i, top):
            here = pl.ds(pl.multiple_of(i * rows, rows), rows)
            s = lax.dot_general(k_ref[here, :], q_ref[...], NT, preferred_element_type=F32)
            prob_ref[here, :] = s
            dprob_ref[here, :] = lax.dot_general(
                v_ref[here, :], g_ref[...], NT, preferred_element_type=F32
            )
            return jnp.maximum(top, jnp.max(s, axis=0, keepdims=True))

        top = lax.fori_loop(0, 2, scores, top)
    power = scale * math.log2(math.e)
    top_ref[...] = top * power
    norm = cross = jnp.zeros((1, rows), F32)
    for _, _, prob_ref, dprob_ref in (near, far):

        def weigh(i, carry):
            norm, cross = carry
            here = pl.ds(pl.multiple_of(i * rows, rows), rows)
            e = jnp.exp2(prob_ref[here, :] * power - top_ref[...])
            prob_ref[here, :] = e
            return (
                norm + jnp.sum(e, axis=0, keepdims=True),
                cross + jnp.sum(e * dprob_ref[here, :], axis=0, keepdims=True),
            )

        norm, cross = lax.fori_loop(0, 2, weigh, (norm, cross))
    inverse = 1.0 / norm
    delta = cross * inverse
    stats_ref[0:1, :] = inverse
    stats_ref[1:2, :] = delta
    dq = jnp.zeros((dim, rows), F32)
    for turn, out_ref in enumerate((stay_ref, send_ref)):
        dkv, part = key_terms(
            scale, turn * rows, rows, q_ref, g_ref, far_k_ref, far_prob_ref, far_dprob_ref, inverse, delta
        )
        out_ref[...] = dkv.astype(out_ref.dtype)
        dq += part
    dq_ref[...] = dq


def attention(qgs, pieces):
    slots, dim = len(qgs), pieces[0][0].shape[1] // 2
    rows = sum(qg.shape[0] for qg in qgs)
    keys, square = ((2 * rows, dim), BF16), ((2 * rows, rows), F32)
    near = [((rows, dim), BF16)] * 2 + [keys, square, square, ((2, rows), F32), ((dim, rows), F32)]
    stay, send, *near = call(
        partial(attention_kernel, 1.0 / math.sqrt(dim), slots),
        "attention",
        [((rows, 2 * dim), F32), ((rows, 2 * dim), BF16), *near],
        [*qgs, *[piece for some in pieces for piece in some]],
        28,
        scratch=[pltpu.VMEM(*kind) for kind in (keys, keys, keys, square, square, ((1, rows), F32))],
    )
    return stay, send, near


def attention_near_kernel(scale, q_ref, g_ref, k_ref, prob_ref, dprob_ref, stats_ref, part_ref, *refs):
    dq_ref, *terms = refs
    rows = q_ref.shape[0]
    dq = part_ref[...]
    for turn, out_ref in enumerate(terms):
        dkv, part = key_terms(
            scale,
            turn * rows,
            rows,
            q_ref,
            g_ref,
            k_ref,
            prob_ref,
            dprob_ref,
            stats_ref[0:1, :],
            stats_ref[1:2, :],
        )
        out_ref[...] = dkv.astype(out_ref.dtype)
        dq += part
    dq_ref[...] = (dq.T * scale).astype(BF16)


def attention_near(near):
    rows, dim = near[0].shape
    return call(
        partial(attention_near_kernel, 1.0 / math.sqrt(dim)),
        "attention_near",
        [((rows, dim), BF16), ((rows, 2 * dim), F32), ((rows, 2 * dim), BF16)],
        near,
        16,
    )


def unfinish_kernel(slots, gain_ref, *refs):
    raws, dqs, dkvs = refs[:slots], refs[slots : 2 * slots], refs[2 * slots : 3 * slots]
    out_ref = refs[-1]
    dim = gain_ref.shape[1]

    def unit_back(raw, gain, upstream):
        hat, scale_back = unit(raw)
        up = upstream.astype(F32) * gain
        return scale_back * (up - hat * jnp.mean(up * hat, axis=-1, keepdims=True))

    for i, (raw, dq, dkv) in enumerate(zip(raws, dqs, dkvs)):
        at = 3 * dim * i
        dq = unit_back(raw[:, :dim], gain_ref[0:1, :], dq[...])
        dk = unit_back(raw[:, dim:], gain_ref[1:2, :], dkv[:, :dim])
        out_ref[:, at : at + dim] = dq.astype(BF16)
        out_ref[:, at + dim : at + 2 * dim] = dk.astype(BF16)
        out_ref[:, at + 2 * dim : at + 3 * dim] = dkv[:, dim:]


def unfinish(gains, raws, dqs, dkvs):
    slots, (rows, dim) = len(dqs), dqs[0].shape
    return call(
        partial(unfinish_kernel, slots),
        "unfinish",
        [((rows, 3 * dim * slots), BF16)],
        (gains, *raws, *dqs, *dkvs),
        6,
    )[0]


def back_project_kernel(grads, *refs):
    weights, out_ref = refs[:-1], refs[-1]
    half = out_ref.shape[1]
    width = grads.shape[1] // len(weights)
    step = half // 7 if half % 7 == 0 else half
    for to in range(0, half, step):
        total = None
        for i, whole in enumerate(weights):
            part = lax.dot_general(
                grads[:, width * i : width * (i + 1)],
                whole[to : to + step, :],
                NT,
                preferred_element_type=F32,
            )
            total = part if total is None else total + part
        out_ref[:, to : to + step] = total.astype(out_ref.dtype)


def back_project(grads, weights, dtype):
    shape = grads.shape[0], weights[0].shape[0]
    return call(back_project_kernel, "back_project", [(shape, dtype)], (grads, *weights), 16)[0]


def close_kernel(own_ref, away_ref, x_ref, c_ref, mod_ref, inv_ref, out_ref):
    half = own_ref.shape[1]
    core = place()[0]
    inv = inv_ref[...]
    total = 0.0
    for i in range(2):
        at = pl.ds(i * half, half)
        grad = jnp.where(core == i, own_ref[...], away_ref[...].astype(F32))
        dhat = grad * (1.0 + mod_ref[1:2, at])
        out_ref[:, at] = dhat
        total += jnp.sum(dhat * x_ref[:, at].astype(F32), axis=-1, keepdims=True)
    cross = total * (inv * inv * (0.5 / half))
    for i in range(2):
        at = pl.ds(i * half, half)
        dhat = out_ref[:, at] - x_ref[:, at].astype(F32) * cross
        out_ref[:, at] = c_ref[:, at].astype(F32) + inv * dhat


def close(own, away, tokens, cotangent, modulation, inv):
    return call(
        close_kernel,
        "close",
        [(tokens.shape, F32)],
        (own, away, tokens, cotangent, modulation, inv),
        12,
    )[0]


def after(value, *earlier):
    return lax.optimization_barrier((value, *earlier))[0]


def weight_gather_body(count, tokens, cotangent, modulation, w_qkv, w_out, qk_gain):
    rows, dim = tokens.shape[0], qk_gain.shape[1]

    def swap(value, pairs):
        return lax.ppermute(value, "seq", pairs)

    w_in = jnp.transpose(w_qkv, (1, 0, 2))
    packed, second = pack(w_in, w_out)
    keep, send, inv = front(after(tokens, packed), cotangent, modulation)
    came, swaps = packed, []
    raws, wholes, heads = [], [], []

    def in_plane(value, axes, pairs, *earlier):
        swaps.append(lax.ppermute(after(value, *swaps[:-2][-1:], *earlier), axes, pairs))
        return swaps[-1]

    def slot(step, blocks, weights, *earlier):
        own, away, whole = project(after(keep, *earlier), come, blocks, weights)
        raw, *head = finish(own, swap(away, CORE_SWAP), qk_gain, step < count - 1)
        wholes.append(whole)
        raws.append(raw)
        heads.append(head)

    def across(value, step):
        pairs = [(4 * t + s, (t + step) % count * 4 + (s ^ 2)) for t in range(count) for s in range(4)]
        return lax.ppermute(value, ("tensor", "seq"), pairs)

    def home(step, *earlier):
        for i, part in enumerate(heads[step]):
            heads[step][i] = around(after(part, *earlier), -step, count)
            earlier = (heads[step][i],)
        return earlier

    for step in range(1, count - 1):
        came = around(came, 1, count)
        if step == 1:
            come = swap(after(send, came), CORE_SWAP)
        one = in_plane(came, PLANE, plane_swap(True), *([keep] if step == 1 else raws[: step - 1]))
        two = in_plane(came, PLANE, plane_swap(False))
        far = in_plane(one, PLANE, plane_swap(False))
        if step == 1:
            slot(0, [], (w_in, w_out))
        slot(step, [came, one, two, far], ())
    near = around(after(packed, *swaps[:1]), -1, count)
    one = in_plane(near, PLANE, plane_swap(True), *raws[: count - 2])
    came = around(after(second, came), -1, count)
    sent = home(1, near)
    far = in_plane(came, PLANE, plane_swap(True), one, *sent)
    for step in range(2, count - 1):
        sent = home(step, *sent)
    slot(count - 1, [near, one, came, far], (), *sent)
    kv, qg = after(heads[-1][0], *sent), after(heads[-1][1], *sent)
    turned = across(kv, 1 - count)
    heads[-1] = [around(kv, 1 - count, count), around(qg, 1 - count, count)]

    kv = jnp.concatenate([head[0][:, : 2 * dim] for head in heads[:-1]], axis=0)
    pieces = [[kv, swap(kv, CORE_SWAP), in_plane(kv, "seq", CHIP_SWAP)]]
    kv = heads[-1][0]
    pieces.append([kv, swap(kv, CORE_SWAP), turned])
    pieces[0][2] = after(pieces[0][2], *heads[-1], turned)
    pieces = [[*four, swap(four[2], CORE_SWAP)] for four in pieces]
    pieces = [[four[i] for four in pieces] for i in range(4)]
    qgs = [head[-1] for head in heads]
    slots = range(count)
    stay, send, near = attention(qgs, pieces)
    far = (stay + swap(send, CORE_SWAP).astype(F32)).astype(BF16)
    dq, stay, send = attention_near(near)
    dq = dq.reshape(count, rows, dim)
    dqs = [around(dq[i], i, count) if i else dq[i] for i in slots]
    summed = stay + swap(send, CORE_SWAP).astype(F32)
    came, *dqs = lax.optimization_barrier((swap(far, CHIP_SWAP), *dqs))
    dkv = (summed + came.astype(F32)).astype(BF16).reshape(count, rows, 2 * dim)
    dkvs = [around(dkv[i], i, count) if i else dkv[i] for i in slots]

    dqkv = unfinish(qk_gain, raws, dqs, dkvs)
    away = swap(back_project(swap(dqkv, CORE_SWAP), wholes, BF16), CORE_SWAP)
    return close(back_project(dqkv, wholes, F32), away, tokens, cotangent, modulation, inv)


def solution(mesh):
    placed = (
        P(("group", "seq", "tensor"), None),
        P(("group", "seq", "tensor"), None),
        P("group", None),
        P(None, None, "tensor"),
        P("tensor", None),
        P(),
    )
    sizes = dict(mesh.shape)

    def body(*args):
        weight_elements = args[3].size + args[4].size
        token_elements = 2 * 3 * args[0].size
        if sizes["group"] == 2 and sizes["seq"] == 4 and weight_elements < token_elements:
            return weight_gather_body(sizes["tensor"], *args)
        return token_gather_body(*args)

    return jax.shard_map(
        body,
        mesh=mesh,
        in_specs=placed,
        out_specs=P(("group", "seq", "tensor"), None),
        check_vma=False,
    )
```
